32 devices in a mesh: stream: 8 (over y, x, core), cross: 4 (over z).
Axes of the slice: x: 2, y: 2, z: 4, core: 2. Of those that a mesh axis runs over, the one named last changes fastest.
Arguments:
- initial_state: float32 [5, 64, 32768], P(None, 'stream', 'cross'), may hold values from -6 to 6
- forcing: float32 [5, 64, 32768], P(None, 'stream', 'cross'), may hold values from -0.3 to 0.3
- block_inverse: float32 [5, 5, 64, 32768], P(None, None, 'stream', 'cross'), may hold values from -1 to 1, as said below
- lower_decay: float32 [5, 64, 32768], P(None, 'stream', 'cross'), may hold values from 0 to 1
- upper_decay: float32 [5, 64, 32768], P(None, 'stream', 'cross'), may hold values from 0 to 1
- cross_coupling: float32 [64, 32768], P('stream', 'cross'), may hold values from 0.002 to 0.02
- iblank: int32 [64, 32768], P('stream', 'cross'), may hold values 0 or 1
- donor_receiver: int32 [1024, 1], P(('stream', 'cross')), may hold values from 0 to 31; in each aligned block of 32 rows (0 to 31, 32 to 63, ...) at most 2 rows name the same one
- donor_block: int32 [1024], P(('stream', 'cross')), may hold values from 0 to 511
- stencil_offset: int32 [1024], P(('stream', 'cross')), may hold values from 1 to 127
- stencil_weight: float32 [1024, 128], P(('stream', 'cross')), may hold values from 0.005 to 0.02
- fringe_target: int32 [2048], P(('stream', 'cross')), may hold values from 0 to 511
Outputs:
- final_state: float32 [5, 64, 32768], P(None, 'stream', 'cross')
- last_update: float32 [5, 64, 32768], P(None, 'stream', 'cross')
The draws below stay inside these ranges and needn't reach their ends.
Inputs may be any that keep to these rules, and one draw needn't show every extreme that they name: `donor_receiver`: within the rows of one device no receiving device is named more than 2 times. `block_inverse`: each 5 x 5 block is orthogonal and symmetric.
All inputs are finite; a program needn't handle non-finite values. No bound on the sum of `iblank` on one device may be relied on, other than what follows from the above.
Results may differ from the reference program's by a relative error of at most 0.00018.
Values sent between devices are 32-bit elements; how exact they have to be, the bound alone decides.
A program may use at most 128 MiB of HBM per device.

```python
import math
import jax
import jax.numpy as jnp
import numpy as np
from jax import lax

CX = 8
CC = 8192
ITERS = 2
CAP = 2
SEND = 32
NX = 64
NC = 32768
NB = 512
N_STREAM = 8
N_CROSS = 4


def draw_block_inverse(key, part):
    vector = jax.random.normal(key, (5, NX, NC), jnp.float32)
    length = jnp.sum(vector * vector, axis=0) + 1e-06
    identity = jnp.eye(5, dtype=jnp.float32)[:, :, None, None]
    return identity - 2.0 * vector[:, None] * vector[None, :] / length[None, None]


def decay_field(key):
    keys = jax.random.split(key, 3)
    low = 0.5 / NX
    high = 1.0 / 30.0
    spread = jax.random.uniform(keys[0], (5, 1, NC), jnp.float32, jnp.log(low), jnp.log(high))
    factor = jnp.broadcast_to(jnp.exp(-jnp.exp(spread)), (5, NX, NC))
    spots = jax.random.randint(keys[1], (3, 5, 1, NC), 0, NX)
    planes = lax.broadcasted_iota(jnp.int32, (5, NX, NC), 1)
    struck = jnp.any(planes[None] == spots, axis=0)
    drop = jax.random.uniform(keys[2], (5, NX, NC), jnp.float32, 0.5, 0.8)
    return jnp.where(struck, factor * drop, factor)


def draw_lower_decay(key, part):
    return decay_field(jax.random.fold_in(key, 11))


def draw_upper_decay(key, part):
    return decay_field(jax.random.fold_in(key, 23))


def plant(entries, rng, least, top_value):
    place = [jax.random.randint(jax.random.fold_in(rng, axis), (), 0, length) for axis, length in enumerate(entries.shape)]
    widest = entries.shape.index(max(entries.shape))
    neighbour = place[:widest] + [(place[widest] + 1) % entries.shape[widest]] + place[widest + 1:]
    return entries.at[tuple(place)].set(least).at[tuple(neighbour)].set(top_value)


def block_levels(rng, extent, shards, smallest, top_value):
    level = 1.0
    for axis_at, shards_of in shards:
        steps = jax.random.uniform(jax.random.fold_in(jax.random.fold_in(rng, 6), axis_at), (shards_of,), jnp.float32, smallest / len(shards), top_value / len(shards))
        level = level * jnp.repeat(jnp.exp(steps), extent[axis_at] // shards_of).reshape((-1,) + (1,) * (len(extent) - 1 - axis_at))
    return level


def shared_out(own_key, own, number, rows, number_of, top, limit, lean):
    order = jax.random.permutation(own_key, number_of)
    packed, common = shares(number_of, rows * top, limit, lean, True), shares(number_of, rows * top, limit, lean, False)
    places = jnp.arange(number_of)

    def named(tallies, turn):
        used = int((tallies > 0).sum())
        fixed = max(1, used // 4)
        passed = fixed + (places - fixed + turn * (used - fixed)) % max(1, number_of - fixed)
        return jnp.zeros((number_of,), jnp.int32).at[order[jnp.where(places < fixed, places, passed)]].set(jnp.asarray(tallies, jnp.int32))

    tallies = jnp.where(number % 4 == 0, named(packed, number // 4), named(common, number - number // 4 - 1))
    mixed = jax.random.permutation(jax.random.fold_in(own, 3), number_of)
    source_of, taker = mixed[0:number_of // 2 * 2:2], mixed[1:number_of // 2 * 2:2]
    slack = jnp.minimum(tallies[source_of] - 1, limit - tallies[taker]) // 2
    slack = jnp.where((source_of == order[0]) | (taker == order[0]) | (tallies[taker] == 0), 0, jnp.maximum(slack, 0))
    passed = jax.random.randint(jax.random.fold_in(own, 4), (number_of // 2,), 0, 1 << 20) % (slack + 1)
    tallies = tallies.at[source_of].add(-passed).at[taker].add(passed)
    labels = jnp.searchsorted(jnp.cumsum(tallies), jnp.arange(rows * top), side="right").astype(jnp.int32)
    listing = labels.reshape(top, rows).T
    listing = listing[jax.random.permutation(jax.random.fold_in(own, 1), rows)]
    turn = jax.random.randint(jax.random.fold_in(own, 2), (rows, 1), 0, top)
    return jnp.take_along_axis(listing, (jnp.arange(top)[None, :] + turn) % top, axis=1)


def shares(amount, total, most, skew, full):
    weights = [(1 << 20) // math.isqrt(rank ** skew) + 1 for rank in range(1, amount + 1)]
    largest = most if full else min(most, max(-(-total // amount), total * weights[0] // sum(weights)))
    least = 1 if total - largest >= amount - 1 else 0
    counts, surplus = [largest] + [least] * (amount - 1), total - largest - least * (amount - 1)
    while surplus > 0:
        candidates = [i for i in range(1, amount) if counts[i] < largest] or [i for i in range(1, amount) if counts[i] < most]
        pool, remaining = sum([weights[i] for i in candidates]), surplus
        for i in candidates:
            extra = min(most - counts[i], max(1, remaining * weights[i] // pool), surplus)
            counts[i] = counts[i] + extra
            surplus = surplus - extra
    return np.array(counts)


def scatter_about(rng, dims, width, bound, pieces=(), held_as=jnp.bfloat16):
    result = width * jax.random.normal(rng, dims, jnp.float32)
    if pieces:
        result = result * block_levels(rng, dims, pieces, -0.22, 0.18)
    return jnp.clip(result, -bound, bound).astype(held_as)


def setup_inputs(seed: int = 0) -> dict:
    key_of = jax.random.split(jax.random.key(seed), 13)
    initial_state = scatter_about(key_of[0], (5, NX, NC), 1.0, 6.0, ((1, 8), (2, 4)), jnp.float32)
    forcing = scatter_about(key_of[1], (5, NX, NC), 0.05, 0.3, ((1, 8), (2, 4)), jnp.float32)
    block_inverse = draw_block_inverse(jax.random.fold_in(key_of[12], 71), 0)
    lower_decay = draw_lower_decay(jax.random.fold_in(key_of[12], 71), 0)
    upper_decay = draw_upper_decay(jax.random.fold_in(key_of[12], 71), 0)
    cross_coupling = jnp.clip(jnp.exp(math.log(0.02) - 2.30258502 * jax.random.uniform(key_of[5], (NX, NC), jnp.float32) ** block_levels(key_of[5], (NX, NC), ((0, 8), (1, 4)), -0.2, 0.2)), 0.002, 0.02)
    iblank = plant((jax.random.randint(key_of[6], (NX, NC), 0, 4) < 3).astype(jnp.int32), jax.random.fold_in(key_of[6], 1), 0, 1)
    donor_receiver_keys = jax.random.split(jax.random.fold_in(key_of[7], 1), (N_STREAM * N_CROSS * SEND) // SEND)
    donor_receiver_turns = jax.random.permutation(jax.random.fold_in(key_of[7], 3), (N_STREAM * N_CROSS * SEND) // SEND)
    donor_receiver = jax.vmap(lambda own, number: shared_out(jax.random.fold_in(key_of[7], 2), own, number, SEND, N_STREAM * N_CROSS, 1, CAP, 2))(donor_receiver_keys, donor_receiver_turns).reshape((N_STREAM * N_CROSS * SEND, 1))
    donor_block = plant(jax.random.randint(key_of[8], (N_STREAM * N_CROSS * SEND,), 0, NB), jax.random.fold_in(key_of[8], 1), 0, NB - 1).astype(jnp.int32)
    stencil_offset = plant(jax.random.randint(key_of[9], (N_STREAM * N_CROSS * SEND,), 1, 128), jax.random.fold_in(key_of[9], 1), 1, 127).astype(jnp.int32)
    stencil_weight = jnp.clip(0.005 + 0.015 * jax.random.uniform(key_of[10], (N_STREAM * N_CROSS * SEND, 128), jnp.float32) ** block_levels(key_of[10], (N_STREAM * N_CROSS * SEND, 128), ((0, 32),), -0.2, 0.2), 0.005, 0.02)
    fringe_target = plant(jax.random.randint(key_of[11], (N_STREAM * N_CROSS * N_STREAM * N_CROSS * CAP,), 0, NB), jax.random.fold_in(key_of[11], 1), 0, NB - 1).astype(jnp.int32)
    return dict(initial_state=initial_state, forcing=forcing, block_inverse=block_inverse, lower_decay=lower_decay, upper_decay=upper_decay, cross_coupling=cross_coupling, iblank=iblank, donor_receiver=donor_receiver, donor_block=donor_block, stencil_offset=stencil_offset, stencil_weight=stencil_weight, fringe_target=fringe_target)


def apply_block(block_inv, vector):
    return jnp.sum(block_inv * vector[None], axis=1)


def fringe_source(state, donor_receiver, donor_block, stencil_offset, stencil_weight, fringe_target):
    devices = N_STREAM * N_CROSS
    block_count = CX * CC // 128
    local = state.reshape(5, N_STREAM, CX, N_CROSS, CC // 128, 128).transpose(1, 3, 0, 2, 4, 5)
    local = local.reshape(devices, 5, block_count, 128)
    rows = devices * SEND
    owner = (jnp.arange(rows, dtype=jnp.int32) // SEND).astype(jnp.int32)
    selected_values = local[owner, :, donor_block]
    lanes = jnp.arange(128, dtype=jnp.int32)[None, :]
    positions = (lanes + stencil_offset[:, None]) % 128
    displaced_values = jnp.take_along_axis(selected_values, jnp.broadcast_to(positions[:, None, :], selected_values.shape), axis=2)
    values = stencil_weight[:, None, :] * (selected_values + displaced_values)
    receiver = donor_receiver[:, 0]
    grouped = receiver.reshape(devices, SEND)
    order = jnp.arange(SEND, dtype=jnp.int32)
    same = grouped[:, :, None] == grouped[:, None, :]
    earlier = order[None, :] < order[:, None]
    slot_rank = jnp.sum((same & earlier[None]).astype(jnp.int32), axis=2).reshape(rows)
    target = fringe_target[receiver * (devices * CAP) + owner * CAP + slot_rank]
    global_block = receiver * block_count + target
    summed = jax.ops.segment_sum(values, global_block, num_segments=devices * block_count)
    summed = summed.reshape(N_STREAM, N_CROSS, CX, CC // 128, 5, 128).transpose(4, 0, 2, 1, 3, 5)
    return summed.reshape(5, NX, NC)


def reference(initial_state, forcing, block_inverse, lower_decay, upper_decay, cross_coupling, iblank, donor_receiver, donor_block, stencil_offset, stencil_weight, fringe_target):
    hole = (1 - iblank).astype(jnp.float32)
    plane_inverses = block_inverse.transpose(2, 0, 1, 3)
    lower_planes = lower_decay.transpose(1, 0, 2)
    upper_planes = upper_decay.transpose(1, 0, 2)

    def forward_step(carry, plane):
        driving_plane, inverse, factor = plane
        near = apply_block(inverse, driving_plane + factor * carry)
        return near, near

    def backward_step(carry, plane):
        near_plane, inverse, factor = plane
        update = near_plane + apply_block(inverse, factor * carry)
        return update, update

    state = initial_state
    update = jnp.zeros_like(initial_state)
    for relaxation_round in range(ITERS):
        laplace = 2.0 * state - jnp.roll(state, 1, axis=2) - jnp.roll(state, -1, axis=2)
        fringe = fringe_source(state, donor_receiver, donor_block, stencil_offset, stencil_weight, fringe_target)
        driving_term = forcing - cross_coupling[None] * laplace + hole[None] * fringe
        start = jnp.zeros((5, NC), jnp.float32)
        _, near = lax.scan(forward_step, start, (driving_term.transpose(1, 0, 2), plane_inverses, lower_planes))
        _, update = lax.scan(backward_step, start, (near, plane_inverses, upper_planes), reverse=True)
        update = update.transpose(1, 0, 2)
        state = state + update
    return state, update
```

```python
import functools

import jax
import jax.numpy as jnp
from jax import lax
from jax.experimental import pallas as pl
from jax.experimental.pallas import tpu as pltpu
from jax.sharding import PartitionSpec as P

ITERS = 2
CAP = 2
NV = 5
SLOT_ROWS = 16
STEP = 16
MATS = NV * NV
MESH = pl.DeviceIdType.MESH
PAIRS = [(a, b) for a in range(NV) for b in range(a, NV)]


def pair(a, b):
    return PAIRS.index((min(a, b), max(a, b)))


def split3(x):
    high = x.astype(jnp.bfloat16)
    rest = x - high.astype(jnp.float32)
    mid = rest.astype(jnp.bfloat16)
    low = (rest - mid.astype(jnp.float32)).astype(jnp.bfloat16)
    return jnp.concatenate([high, mid, low], axis=0)


def iota(shape, dim):
    return lax.broadcasted_iota(jnp.int32, shape, dim)


def kernel(
    ns, nc, planes, tiles,
    state_h, forcing_h, inverse_h, lower_h, upper_h, coupling_h, blank_h,
    receiver_r, block_s, offset_r, weight_r, target_r,
    final_h, update_h,
    state, forcing, inverse, lower, upper, coupling, blank,
    drive, near, update, gathered, placed, outgoing, received, pick, stacked,
    edge_out, edge_in,
    stage, mats, comp, prev_a, next_e,
    zero, chip_b, chip_c, prev_b, x_in, x_out, x_face, g_own, g_in, y_in, y_out, y_face,
    load_sem, out_sem, fsend, frecv, esend, erecv, msend, mrecv, csend, crecv,
):
    s, c = lax.axis_index("stream"), lax.axis_index("cross")
    devices = ns * nc
    me = s * nc + c
    senders = block_s.shape[0]
    slots = devices * CAP
    groups = ns // 2
    half = tiles // 2
    core = lax.rem(s, 2)
    group = s // 2
    odd = lax.rem(group, 2) == 1
    own_base = lax.rem(core + group, 2) * half
    far_base = half - own_base

    loads = []

    def load(source, target):
        copy = pltpu.make_async_copy(source, target, load_sem.at[len(loads)])
        copy.start()
        loads.append(copy)
        return copy

    def rows_of(i):
        return pl.ds(i * tiles, tiles)

    state_loads = [load(state_h.at[:, :, i, :], state.at[:, rows_of(i), :]) for i in range(planes)]
    sweep_loads = []
    for i in range(planes):
        sweep_loads.append(load(lower_h.at[:, :, i, :], lower.at[:, rows_of(i), :]))
        for a in range(NV):
            first = pair(a, a)
            sweep_loads.append(
                load(
                    inverse_h.at[a, pl.ds(a, NV - a), :, i, :],
                    inverse.at[pl.ds(first, NV - a), rows_of(i), :],
                )
            )
    for i in range(planes):
        sweep_loads.append(load(upper_h.at[:, :, i, :], upper.at[:, rows_of(i), :]))
    drive_loads = []
    for i in range(planes):
        drive_loads.append(load(forcing_h.at[:, :, i, :], forcing.at[:, rows_of(i), :]))
        drive_loads.append(load(coupling_h.at[:, i, :], coupling.at[rows_of(i), :]))
        drive_loads.append(load(blank_h.at[:, i, :], blank.at[rows_of(i), :]))

    barrier = pltpu.get_barrier_semaphore()

    def greet(k, carry):
        other = lax.rem(me + k, devices)
        pl.semaphore_signal(
            barrier, inc=1, device_id=(other // nc, lax.rem(other, nc)), device_id_type=MESH
        )
        return carry

    lax.fori_loop(1, devices, greet, 0)

    eye = iota((senders, senders), 0) == iota((senders, senders), 1)
    recv_row = receiver_r[...].astype(jnp.float32)
    recv_col = jnp.sum(jnp.where(eye, recv_row, 0.0), axis=1, keepdims=True)
    earlier = iota((senders, senders), 0) < iota((senders, senders), 1)
    rank_row = jnp.sum(
        jnp.where(earlier & (recv_col == recv_row), 1.0, 0.0), axis=0, keepdims=True
    )
    key_row = rank_row * devices + recv_row
    place = (key_row == iota((slots, senders), 0).astype(jnp.float32)).astype(jnp.float32)
    place3 = jnp.concatenate([place, place, place], axis=1).astype(jnp.bfloat16)
    offset_col = jnp.sum(
        jnp.where(eye, offset_r[...].astype(jnp.float32), 0.0), axis=1, keepdims=True
    ).astype(jnp.int32)
    offset_all = jnp.broadcast_to(offset_col, (senders, 128))

    def fill_pick():
        slot_eye = iota((slots, slots), 0) == iota((slots, slots), 1)
        target_col = jnp.sum(
            jnp.where(slot_eye, target_r[...].astype(jnp.float32), 0.0), axis=1, keepdims=True
        )
        slot_k = iota((slots, slots), 1)
        wanted = jnp.where(slot_k < devices, slot_k * CAP, (slot_k - devices) * CAP + 1)
        target_row = jnp.sum(
            jnp.where(iota((slots, slots), 0) == wanted, target_col, 0.0), axis=0, keepdims=True
        )
        target3 = jnp.concatenate([target_row, target_row, target_row], axis=1)

        def fill(i, carry):
            ids = (iota((tiles, 3 * slots), 0) + i * tiles).astype(jnp.float32)
            pick[pl.ds(pl.multiple_of(i * tiles, tiles), tiles), :] = jnp.where(
                ids == target3, 1.0, 0.0
            ).astype(jnp.bfloat16)
            return carry

        lax.fori_loop(0, planes, fill, 0)

    for copy in state_loads:
        copy.wait()
    pl.semaphore_wait(barrier, devices - 1)

    def fringe_copy(it, k):
        other = lax.rem(me + k, devices)
        start = pl.multiple_of(other * SLOT_ROWS, SLOT_ROWS)
        mine = pl.multiple_of(me * SLOT_ROWS, SLOT_ROWS)
        return pltpu.make_async_remote_copy(
            src_ref=outgoing.at[it, pl.ds(start, NV * CAP), :],
            dst_ref=received.at[it, pl.ds(mine, NV * CAP), :],
            send_sem=fsend.at[it, k],
            recv_sem=frecv.at[it, k],
            device_id=(other // nc, lax.rem(other, nc)),
            device_id_type=MESH,
        )

    def edge_copy(it, side):
        other = lax.rem(c + 1, nc) if side == 0 else lax.rem(c + nc - 1, nc)
        return pltpu.make_async_remote_copy(
            src_ref=edge_out.at[it, side],
            dst_ref=edge_in.at[it, side],
            send_sem=esend.at[it, side],
            recv_sem=erecv.at[it, side],
            device_id=(s, other),
            device_id_type=MESH,
        )

    def member(other_group, across):
        return other_group * 2 + (1 - core if across else core)

    partner = member(group, True)

    def face_copy(it, kind, way, source, target, to):
        return pltpu.make_async_remote_copy(
            src_ref=source,
            dst_ref=target,
            send_sem=csend.at[it, way],
            recv_sem=crecv.at[it, kind],
            device_id=(to, c),
            device_id_type=MESH,
        )

    def mats_copy(k):
        third = pl.ds(k * MATS, MATS)
        return pltpu.make_async_remote_copy(
            src_ref=mats.at[2, third],
            dst_ref=mats.at[core, third],
            send_sem=msend.at[k],
            recv_sem=mrecv.at[k],
            device_id=(partner, c),
            device_id_type=MESH,
        )

    def prev_a_copy():
        return pltpu.make_async_remote_copy(
            src_ref=comp.at[pl.ds(0, MATS)],
            dst_ref=prev_a,
            send_sem=msend.at[3],
            recv_sem=mrecv.at[3],
            device_id=(member(group + 1, True), c),
            device_id_type=MESH,
        )

    def next_e_copy():
        return pltpu.make_async_remote_copy(
            src_ref=comp.at[pl.ds(MATS, MATS)],
            dst_ref=next_e,
            send_sem=msend.at[4],
            recv_sem=mrecv.at[4],
            device_id=(member(group - 1, True), c),
            device_id_type=MESH,
        )

    def b_to_partner(it):
        return face_copy(it, 0, 0, zero.at[it, 2, 0], zero.at[it, core, 0], partner)

    def c_to_partner(it):
        return face_copy(it, 1, 1, zero.at[it, 2, 1], zero.at[it, core, 1], partner)

    def b_to_next(it):
        return face_copy(it, 2, 2, chip_b.at[it], prev_b.at[it], member(group + 1, True))

    def x_to_next(it):
        return face_copy(it, 3, 3, x_out.at[it], x_in.at[it], member(group + 1, True))

    def x_to_skip(it):
        return face_copy(it, 3, 4, x_out.at[it], x_in.at[it], member(group + 2, False))

    def g_to_prev(it):
        return face_copy(it, 4, 5, g_own.at[it], g_in.at[it], member(group - 1, True))

    def y_to_prev(it):
        return face_copy(it, 5, 6, y_out.at[it], y_in.at[it], member(group - 1, True))

    def y_to_skip(it):
        return face_copy(it, 5, 7, y_out.at[it], y_in.at[it], member(group - 2, False))

    own_rows = pl.ds(pl.multiple_of(own_base, half), half)

    def x_to_partner(it):
        source = x_face.at[it, 1 - core, :, own_rows, :]
        return face_copy(it, 6, 8, source, source, partner)

    def y_to_partner(it):
        source = y_face.at[it, 1 - core, :, own_rows, :]
        return face_copy(it, 7, 9, source, source, partner)

    def block(rows):
        return [inverse[k, rows, :] for k in range(len(PAIRS))]

    def dot(terms):
        total = None
        for left, right in terms:
            total = left * right if total is None else total + left * right
        return total

    def apply(blocks, vector):
        return [dot([(blocks[pair(a, b)], vector[b]) for b in range(NV)]) for a in range(NV)]

    def at(base, size):
        return pl.ds(pl.multiple_of(base, 8), size)

    def matrix(ref, first, rows):
        return [[ref[first + a * NV + b, rows, :] for b in range(NV)] for a in range(NV)]

    def times(rows_of_matrix, vector):
        return [dot([(rows_of_matrix[a][b], vector[b]) for b in range(NV)]) for a in range(NV)]

    def column(m, b):
        return [m[a][b] for a in range(NV)]

    def transfer(q, carry):
        each = half // 8
        local = lax.rem(q, each) * 8
        base = jnp.where(q < each, far_base, own_base) + local
        slot = jnp.where(q < each, 2, core)
        spot = at(local, 8)
        chain = None
        for i in range(planes):
            rows = at(i * tiles + base, 8)
            blocks = block(rows)
            factor = [lower[v, rows, :] for v in range(NV)]
            if i == 0:
                chain = [[blocks[pair(a, b)] * factor[b] for a in range(NV)] for b in range(NV)]
            else:
                chain = [
                    apply(blocks, [factor[v] * chain[b][v] for v in range(NV)]) for b in range(NV)
                ]
            for b in range(NV):
                for a in range(NV):
                    stage[i, a * NV + b] = chain[b][a]
        for b in range(NV):
            for a in range(NV):
                mats[slot, a * NV + b, spot, :] = chain[b][a]
        both = chain
        for i in reversed(range(planes - 1)):
            rows = at(i * tiles + base, 8)
            blocks = block(rows)
            factor = [upper[v, rows, :] for v in range(NV)]
            both = [
                [
                    stage[i, a * NV + b] + z
                    for a, z in enumerate(apply(blocks, [factor[v] * both[b][v] for v in range(NV)]))
                ]
                for b in range(NV)
            ]
        for b in range(NV):
            for a in range(NV):
                mats[slot, 2 * MATS + a * NV + b, spot, :] = both[b][a]
        back = None
        for i in reversed(range(planes)):
            rows = at(i * tiles + base, 8)
            blocks = block(rows)
            factor = [upper[v, rows, :] for v in range(NV)]
            if i == planes - 1:
                back = [[blocks[pair(a, b)] * factor[b] for a in range(NV)] for b in range(NV)]
            else:
                back = [
                    apply(blocks, [factor[v] * back[b][v] for v in range(NV)]) for b in range(NV)
                ]
        for b in range(NV):
            for a in range(NV):
                mats[slot, MATS + a * NV + b, spot, :] = back[b][a]

        @pl.when(q == each - 1)
        def _():
            for k in range(3):
                mats_copy(k).start()

        return carry

    def compose(q, carry):
        rows = at(q * 8, 8)
        low_a = matrix(mats.at[0], 0, rows)
        high_a = matrix(mats.at[1], 0, rows)
        for b in range(NV):
            out = times(high_a, column(low_a, b))
            for a in range(NV):
                comp[a * NV + b, rows, :] = out[a]
        low_e = matrix(mats.at[0], MATS, rows)
        high_e = matrix(mats.at[1], MATS, rows)
        for b in range(NV):
            out = times(low_e, column(high_e, b))
            for a in range(NV):
                comp[MATS + a * NV + b, rows, :] = out[a]
        high_d = matrix(mats.at[1], 2 * MATS, rows)
        for b in range(NV):
            inner = times(high_d, column(low_a, b))
            out = times(low_e, inner)
            for a in range(NV):
                k = 2 * MATS + a * NV + b
                comp[k, rows, :] = mats[0, k, rows, :] + out[a]
        return carry

    def zero_down(it, base, slot):
        for g in range(half // STEP):
            x = None
            for i in range(planes):
                rows = at(i * tiles + base + g * STEP, STEP)
                t = [drive[v, rows, :] for v in range(NV)]
                if x is not None:
                    t = [t[v] + lower[v, rows, :] * x[v] for v in range(NV)]
                x = apply(block(rows), t)
                for v in range(NV):
                    near[v, rows, :] = x[v]
            for v in range(NV):
                zero[it, slot, 0, v, pl.ds(g * STEP, STEP), :] = x[v]

    def zero_up(it, base, slot):
        for g in range(half // STEP):
            rows = at((planes - 1) * tiles + base + g * STEP, STEP)
            y = [near[v, rows, :] for v in range(NV)]
            for i in reversed(range(planes - 1)):
                rows = at(i * tiles + base + g * STEP, STEP)
                z = apply(block(rows), [upper[v, rows, :] * y[v] for v in range(NV)])
                y = [near[v, rows, :] + z[v] for v in range(NV)]
            for v in range(NV):
                zero[it, slot, 1, v, pl.ds(g * STEP, STEP), :] = y[v]

    def true_down(it, base):
        for g in range(half // STEP):
            x = [x_face[it, core, v, at(base + g * STEP, STEP), :] for v in range(NV)]
            for i in range(planes):
                rows = at(i * tiles + base + g * STEP, STEP)
                t = [drive[v, rows, :] + lower[v, rows, :] * x[v] for v in range(NV)]
                x = apply(block(rows), t)
                for v in range(NV):
                    near[v, rows, :] = x[v]

    def true_up(it, base):
        for g in range(half // STEP):
            y = [y_face[it, core, v, at(base + g * STEP, STEP), :] for v in range(NV)]
            for i in reversed(range(planes)):
                rows = at(i * tiles + base + g * STEP, STEP)
                z = apply(block(rows), [upper[v, rows, :] * y[v] for v in range(NV)])
                y = [near[v, rows, :] + z[v] for v in range(NV)]
                for v in range(NV):
                    if it == ITERS - 1:
                        update[v, rows, :] = y[v]
                    state[v, rows, :] = state[v, rows, :] + y[v]

    def out_copies(part, base):
        copies = []
        for i in range(planes):
            rows = pl.ds(pl.multiple_of(i * tiles + base, half), half)
            cells = pl.ds(pl.multiple_of(base, half), half)
            for n, (source, target) in enumerate(((state, final_h), (update, update_h))):
                copies.append(
                    pltpu.make_async_copy(
                        source.at[:, rows, :], target.at[:, cells, i, :], out_sem.at[part, i, n]
                    )
                )
        return copies

    steps = [pl.ds(g * STEP, STEP) for g in range(half // STEP)]

    def chip_forward(it):
        for rows in steps:
            low = [zero[it, 0, 0, v, rows, :] for v in range(NV)]
            out = times(matrix(mats.at[1], 0, rows), low)
            for v in range(NV):
                chip_b[it, v, rows, :] = zero[it, 1, 0, v, rows, :] + out[v]

    def chip_backward(it):
        for rows in steps:
            low = [zero[it, 0, 0, v, rows, :] for v in range(NV)]
            out = times(matrix(mats.at[1], 2 * MATS, rows), low)
            out = [out[v] + zero[it, 1, 1, v, rows, :] for v in range(NV)]
            out = times(matrix(mats.at[0], MATS, rows), out)
            for v in range(NV):
                chip_c[it, v, rows, :] = zero[it, 0, 1, v, rows, :] + out[v]

    def own(g):
        return at(own_base + g * STEP, STEP)

    def relay_forward(it):
        for g, rows in enumerate(steps):
            out = times(matrix(prev_a, 0, rows), [x_in[it, v, rows, :] for v in range(NV)])
            x = [prev_b[it, v, rows, :] + out[v] for v in range(NV)]
            out = times(matrix(comp, 0, rows), x)
            for v in range(NV):
                x_out[it, v, rows, :] = chip_b[it, v, rows, :] + out[v]
                x_face[it, 0, v, own(g), :] = x[v]

    def turn(it):
        for g, rows in enumerate(steps):
            x = [x_face[it, 0, v, own(g), :] for v in range(NV)]
            out = times(matrix(comp, 2 * MATS, rows), x)
            for v in range(NV):
                g_own[it, v, rows, :] = chip_c[it, v, rows, :] + out[v]

    def inner_forward(it):
        for g, rows in enumerate(steps):
            x = [x_face[it, 0, v, own(g), :] for v in range(NV)]
            out = times(matrix(mats.at[0], 0, rows), x)
            for v in range(NV):
                x_face[it, 1, v, own(g), :] = zero[it, 0, 0, v, rows, :] + out[v]

    def relay_backward(it):
        for g, rows in enumerate(steps):
            out = times(matrix(next_e, 0, rows), [y_in[it, v, rows, :] for v in range(NV)])
            y = [g_in[it, v, rows, :] + out[v] for v in range(NV)]
            out = times(matrix(comp, MATS, rows), y)
            for v in range(NV):
                y_out[it, v, rows, :] = g_own[it, v, rows, :] + out[v]
                y_face[it, 1, v, own(g), :] = y[v]

    def inner_backward(it):
        for g, rows in enumerate(steps):
            x = [x_face[it, 1, v, own(g), :] for v in range(NV)]
            out = times(matrix(mats.at[1], 2 * MATS, rows), x)
            y = [y_face[it, 1, v, own(g), :] for v in range(NV)]
            back = times(matrix(mats.at[1], MATS, rows), y)
            for v in range(NV):
                y_face[it, 0, v, own(g), :] = zero[it, 1, 1, v, rows, :] + out[v] + back[v]

    face_zero = jnp.zeros((NV, half, 128), jnp.float32)

    @pl.when(group == 1)
    def _():
        prev_a[...] = jnp.zeros((MATS, half, 128), jnp.float32)
        for it in range(ITERS):
            x_in[it] = face_zero

    @pl.when(group == groups - 1)
    def _():
        next_e[...] = jnp.zeros((MATS, half, 128), jnp.float32)
        for it in range(ITERS):
            y_in[it] = face_zero
            g_in[it] = face_zero

    for it in range(ITERS):
        for v in range(NV):
            edge_out[it, 0, v] = state[v, pl.ds(tiles - 1, planes, stride=tiles), :]
            edge_out[it, 1, v] = state[v, pl.ds(0, planes, stride=tiles), :]
        for side in range(2):
            edge_copy(it, side).start()

        def gather(q, carry):
            for k in range(8):
                e = q * 8 + k
                chosen = block_s[e]
                for v in range(NV):
                    gathered[v, pl.ds(e, 1), :] = state[v, pl.ds(chosen, 1), :]
            return carry

        lax.fori_loop(0, senders // 8, gather, 0)
        weight = weight_r[...]
        for v in range(NV):
            chosen = gathered[v]
            moved = chosen
            for bit in range(7):
                rolled = pltpu.roll(moved, 128 - (1 << bit), 1)
                moved = jnp.where((offset_all & (1 << bit)) != 0, rolled, moved)
            placed[:, v * 128:(v + 1) * 128] = split3(weight * (chosen + moved))
        slot_values = jnp.dot(place3, placed[...], preferred_element_type=jnp.float32)
        for v in range(NV):
            for k in range(CAP):
                outgoing[it, pl.ds(v * CAP + k, devices, stride=SLOT_ROWS), :] = slot_values[
                    k * devices:(k + 1) * devices, v * 128:(v + 1) * 128
                ]

        def send(k, carry):
            fringe_copy(it, k).start()
            return carry

        lax.fori_loop(1, devices, send, 0)
        mine = pl.ds(pl.multiple_of(me * SLOT_ROWS, SLOT_ROWS), NV * CAP)
        received[it, mine, :] = outgoing[it, mine, :]

        if it == 0:
            fill_pick()
            for copy in sweep_loads:
                copy.wait()
            lax.fori_loop(0, tiles // 8, transfer, 0)
            for copy in drive_loads:
                copy.wait()
        for side in range(2):
            edge_copy(it, side).wait_recv()
        lane = iota((tiles, 128), 1)
        row = iota((tiles, 128), 0)

        def drive_plane(i, carry):
            rows = pl.ds(pl.multiple_of(i * tiles, tiles), tiles)
            factor = coupling[rows, :]
            for v in range(NV):
                x = state[v, rows, :]
                before = pltpu.roll(edge_in[it, 0, v, pl.ds(i, 1), :], 1, 1)
                after = pltpu.roll(edge_in[it, 1, v, pl.ds(i, 1), :], 127, 1)
                left = pltpu.roll(x, 1, 1)
                left = jnp.where(
                    lane == 0, jnp.where(row == 0, before, pltpu.roll(left, 1, 0)), left
                )
                right = pltpu.roll(x, 127, 1)
                right = jnp.where(
                    lane == 127,
                    jnp.where(row == tiles - 1, after, pltpu.roll(right, tiles - 1, 0)),
                    right,
                )
                drive[v, rows, :] = forcing[v, rows, :] - factor * (2.0 * x - left - right)
            return carry

        lax.fori_loop(0, planes, drive_plane, 0)

        def take(k, carry):
            fringe_copy(it, k).wait_recv()
            return carry

        lax.fori_loop(1, devices, take, 0)
        for v in range(NV):
            parts = [
                received[it, pl.ds(v * CAP + k, devices, stride=SLOT_ROWS), :] for k in range(CAP)
            ]
            stacked[:, v * 128:(v + 1) * 128] = split3(jnp.concatenate(parts, axis=0))

        def add_fringe(i, carry):
            rows = pl.ds(pl.multiple_of(i * tiles, tiles), tiles)
            hole = (1 - blank[rows, :]).astype(jnp.float32)
            fringe = jnp.dot(pick[rows, :], stacked[...], preferred_element_type=jnp.float32)
            for v in range(NV):
                drive[v, rows, :] = drive[v, rows, :] + hole * fringe[:, v * 128:(v + 1) * 128]
            return carry

        lax.fori_loop(0, planes, add_fringe, 0)

        zero_down(it, far_base, 2)
        b_to_partner(it).start()
        zero_down(it, own_base, core)
        zero_up(it, far_base, 2)
        c_to_partner(it).start()
        zero_up(it, own_base, core)

        if it == 0:
            for k in range(3):
                mats_copy(k).wait_recv()
        b_to_partner(it).wait_recv()
        chip_forward(it)

        @pl.when(jnp.logical_not(odd))
        def _():
            b_to_next(it).start()

        if it == 0:
            lax.fori_loop(0, half // 8, compose, 0)

            @pl.when(jnp.logical_not(odd) & (group > 0))
            def _():
                prev_a_copy().start()
                next_e_copy().start()

        c_to_partner(it).wait_recv()
        chip_backward(it)

        @pl.when(odd)
        def _():
            b_to_next(it).wait_recv()

            @pl.when(group > 1)
            def _():
                if it == 0:
                    prev_a_copy().wait_recv()
                x_to_skip(it).wait_recv()

            relay_forward(it)

            @pl.when(group < groups - 1)
            def _():
                x_to_skip(it).start()
                x_to_next(it).start()

        @pl.when(jnp.logical_not(odd))
        def _():
            @pl.when(group > 0)
            def _():
                x_to_next(it).wait_recv()
                x_face[it, 0, :, own_rows, :] = x_in[it]

            @pl.when(group == 0)
            def _():
                x_face[it, 0, :, own_rows, :] = face_zero

        turn(it)

        @pl.when(jnp.logical_not(odd) & (group > 0))
        def _():
            g_to_prev(it).start()

        def pass_back():
            relay_backward(it)
            y_to_prev(it).start()

            @pl.when(group > 1)
            def _():
                y_to_skip(it).start()

        @pl.when(group == groups - 1)
        def _():
            pass_back()

        inner_forward(it)
        x_to_partner(it).start()
        true_down(it, own_base)
        x_to_partner(it).wait_recv()
        true_down(it, far_base)

        @pl.when(odd & (group < groups - 1))
        def _():
            g_to_prev(it).wait_recv()
            if it == 0:
                next_e_copy().wait_recv()
            y_to_skip(it).wait_recv()
            pass_back()

        @pl.when(jnp.logical_not(odd))
        def _():
            y_to_prev(it).wait_recv()
            y_face[it, 1, :, own_rows, :] = y_in[it]

        inner_backward(it)
        y_to_partner(it).start()
        true_up(it, own_base)
        if it == ITERS - 1:
            for copy in out_copies(0, own_base):
                copy.start()
        y_to_partner(it).wait_recv()
        true_up(it, far_base)
        if it == ITERS - 1:
            for copy in out_copies(1, far_base):
                copy.start()

    for k in range(3):
        mats_copy(k).wait_send()

    @pl.when(jnp.logical_not(odd) & (group > 0))
    def _():
        prev_a_copy().wait_send()
        next_e_copy().wait_send()

    for it in range(ITERS):
        for side in range(2):
            edge_copy(it, side).wait_send()

        def sent(k, carry):
            fringe_copy(it, k).wait_send()
            return carry

        lax.fori_loop(1, devices, sent, 0)
        b_to_partner(it).wait_send()
        c_to_partner(it).wait_send()
        x_to_partner(it).wait_send()
        y_to_partner(it).wait_send()

        @pl.when(jnp.logical_not(odd))
        def _():
            b_to_next(it).wait_send()

            @pl.when(group > 0)
            def _():
                g_to_prev(it).wait_send()

        @pl.when(odd)
        def _():
            y_to_prev(it).wait_send()

            @pl.when(group > 1)
            def _():
                y_to_skip(it).wait_send()

            @pl.when(group < groups - 1)
            def _():
                x_to_skip(it).wait_send()
                x_to_next(it).wait_send()

    for part, base in enumerate((own_base, far_base)):
        for copy in out_copies(part, base):
            copy.wait()


def shards(
    initial_state, forcing, block_inverse, lower_decay, upper_decay, cross_coupling, iblank,
    donor_receiver, donor_block, stencil_offset, stencil_weight, fringe_target,
):
    ns, nc = lax.axis_size("stream"), lax.axis_size("cross")
    devices = ns * nc
    planes, cells = initial_state.shape[1:]
    tiles = cells // 128
    senders = donor_block.shape[0]
    slots = devices * CAP

    def tiled(x):
        lead = x.shape[:-2]
        n = len(lead)
        order = tuple(range(n)) + (n + 1, n, n + 2)
        return x.reshape(lead + (planes, tiles, 128)).transpose(order)

    def untiled(x):
        return x.transpose(0, 2, 1, 3).reshape(NV, planes, cells)

    full = (NV, planes * tiles, 128)
    half = tiles // 2
    f32, bf16 = jnp.float32, jnp.bfloat16
    dma = pltpu.SemaphoreType.DMA
    face = pltpu.VMEM((ITERS, NV, half, 128), f32)
    out = jax.ShapeDtypeStruct((NV, tiles, planes, 128), f32)
    hbm = pl.BlockSpec(memory_space=pl.ANY)
    vmem = pl.BlockSpec(memory_space=pltpu.VMEM)
    smem = pl.BlockSpec(memory_space=pltpu.SMEM)
    final, update = pl.pallas_call(
        functools.partial(kernel, ns, nc, planes, tiles),
        out_shape=(out, out),
        in_specs=[hbm] * 7 + [vmem, smem, vmem, vmem, vmem],
        out_specs=(hbm, hbm),
        scratch_shapes=[
            pltpu.VMEM(full, f32),
            pltpu.VMEM(full, f32),
            pltpu.VMEM((len(PAIRS),) + full[1:], f32),
            pltpu.VMEM(full, f32),
            pltpu.VMEM(full, f32),
            pltpu.VMEM(full[1:], f32),
            pltpu.VMEM(full[1:], jnp.int32),
            pltpu.VMEM(full, f32),
            pltpu.VMEM(full, f32),
            pltpu.VMEM(full, f32),
            pltpu.VMEM((NV, senders, 128), f32),
            pltpu.VMEM((3 * senders, NV * 128), bf16),
            pltpu.VMEM((ITERS, devices * SLOT_ROWS, 128), f32),
            pltpu.VMEM((ITERS, devices * SLOT_ROWS, 128), f32),
            pltpu.VMEM((planes * tiles, 3 * slots), bf16),
            pltpu.VMEM((3 * slots, NV * 128), bf16),
            pltpu.VMEM((ITERS, 2, NV, planes, 128), f32),
            pltpu.VMEM((ITERS, 2, NV, planes, 128), f32),
            pltpu.VMEM((planes, MATS, 8, 128), f32),
            pltpu.VMEM((3, 3 * MATS, half, 128), f32),
            pltpu.VMEM((3 * MATS, half, 128), f32),
            pltpu.VMEM((MATS, half, 128), f32),
            pltpu.VMEM((MATS, half, 128), f32),
            pltpu.VMEM((ITERS, 3, 2, NV, half, 128), f32),
            face,
            face,
            face,
            face,
            face,
            pltpu.VMEM((ITERS, 2, NV, tiles, 128), f32),
            face,
            face,
            face,
            face,
            pltpu.VMEM((ITERS, 2, NV, tiles, 128), f32),
            dma((planes * (4 + 2 + NV),)),
            dma((2, planes, 2)),
            dma((ITERS, devices)),
            dma((ITERS, devices)),
            dma((ITERS, 2)),
            dma((ITERS, 2)),
            dma((5,)),
            dma((5,)),
            dma((ITERS, 10)),
            dma((ITERS, 8)),
        ],
        compiler_params=pltpu.CompilerParams(
            collective_id=0, has_side_effects=True, vmem_limit_bytes=56 * 1024 * 1024
        ),
    )(
        tiled(initial_state), tiled(forcing), tiled(block_inverse), tiled(lower_decay),
        tiled(upper_decay), tiled(cross_coupling), tiled(iblank),
        donor_receiver.reshape(1, senders), donor_block, stencil_offset.reshape(1, senders), stencil_weight,
        fringe_target.reshape(1, slots),
    )
    return untiled(final), untiled(update)


def solution(mesh):
    return jax.shard_map(
        shards,
        mesh=mesh,
        in_specs=(
            P(None, "stream", "cross"),
            P(None, "stream", "cross"),
            P(None, None, "stream", "cross"),
            P(None, "stream", "cross"),
            P(None, "stream", "cross"),
            P("stream", "cross"),
            P("stream", "cross"),
            P(("stream", "cross"), None),
            P(("stream", "cross")),
            P(("stream", "cross")),
            P(("stream", "cross"), None),
            P(("stream", "cross")),
        ),
        out_specs=(P(None, "stream", "cross"), P(None, "stream", "cross")),
        check_vma=False,
    )
```

```python
import functools

import jax
import jax.numpy as jnp
from jax import lax
from jax.experimental import pallas as pl
from jax.experimental.pallas import tpu as pltpu
from jax.sharding import PartitionSpec as P

ITERS = 2
CAP = 2
NV = 5
SLOT_ROWS = 16
STEP = 16
PART = 8
MATS = NV * NV
BATCHES = ((0, 1, 2, 3, 4),)
MESH = pl.DeviceIdType.MESH
PAIRS = [(a, b) for a in range(NV) for b in range(a, NV)]


def pair(a, b):
    return PAIRS.index((min(a, b), max(a, b)))


def split3(x):
    high = x.astype(jnp.bfloat16)
    rest = x - high.astype(jnp.float32)
    mid = rest.astype(jnp.bfloat16)
    low = (rest - mid.astype(jnp.float32)).astype(jnp.bfloat16)
    return jnp.concatenate([high, mid, low], axis=0)


def iota(shape, dim):
    return lax.broadcasted_iota(jnp.int32, shape, dim)


def kernel(
    ns, nc, planes, tiles,
    state_h, forcing_h, inverse_h, lower_h, upper_h, coupling_h, blank_h,
    receiver_r, block_s, offset_r, weight_r, target_r,
    final_h, update_h,
    state, forcing, inverse, lower, upper, coupling, blank,
    drive, near, update, gathered, placed, outgoing, received, pick, stacked,
    edge_out, edge_in,
    stage, mats, comp,
    zero, chip_b, chip_c, x_in, x_out, x_face, g_own, g_inner, y_in, y_out, y_face,
    load_sem, out_sem, fsend, frecv, esend, erecv, msend, mrecv, csend, crecv,
):
    s, c = lax.axis_index("stream"), lax.axis_index("cross")
    devices = ns * nc
    me = s * nc + c
    senders = block_s.shape[0]
    slots = devices * CAP
    groups = ns // 2
    half = tiles // 2
    core = lax.rem(s, 2)
    group = s // 2
    first, last = group == 0, group == groups - 1
    own_base = lax.rem(core + group, 2) * half
    far_base = half - own_base

    loads = []

    def load(source, target):
        copy = pltpu.make_async_copy(source, target, load_sem.at[len(loads)])
        copy.start()
        loads.append(copy)
        return copy

    def rows_of(i):
        return pl.ds(i * tiles, tiles)

    sweep_loads = []
    for i in range(planes):
        sweep_loads.append(load(lower_h.at[:, :, i, :], lower.at[:, rows_of(i), :]))
        for a in range(NV):
            top = pair(a, a)
            sweep_loads.append(
                load(
                    inverse_h.at[a, pl.ds(a, NV - a), :, i, :],
                    inverse.at[pl.ds(top, NV - a), rows_of(i), :],
                )
            )
    for i in range(planes):
        sweep_loads.append(load(upper_h.at[:, :, i, :], upper.at[:, rows_of(i), :]))
    barrier = pltpu.get_barrier_semaphore()

    def greet(k, carry):
        other = lax.rem(me + k, devices)
        pl.semaphore_signal(
            barrier, inc=1, device_id=(other // nc, lax.rem(other, nc)), device_id_type=MESH
        )
        return carry

    lax.fori_loop(1, devices, greet, 0)

    state_loads = [load(state_h.at[:, :, i, :], state.at[:, rows_of(i), :]) for i in range(planes)]
    drive_loads = []
    for i in range(planes):
        drive_loads.append(load(forcing_h.at[:, :, i, :], forcing.at[:, rows_of(i), :]))
        drive_loads.append(load(coupling_h.at[:, i, :], coupling.at[rows_of(i), :]))
        drive_loads.append(load(blank_h.at[:, i, :], blank.at[rows_of(i), :]))

    eye = iota((senders, senders), 0) == iota((senders, senders), 1)
    recv_row = receiver_r[...].astype(jnp.float32)
    recv_col = jnp.sum(jnp.where(eye, recv_row, 0.0), axis=1, keepdims=True)
    earlier = iota((senders, senders), 0) < iota((senders, senders), 1)
    rank_row = jnp.sum(
        jnp.where(earlier & (recv_col == recv_row), 1.0, 0.0), axis=0, keepdims=True
    )
    key_row = rank_row * devices + recv_row
    place = (key_row == iota((slots, senders), 0).astype(jnp.float32)).astype(jnp.float32)
    place3 = jnp.concatenate([place, place, place], axis=1).astype(jnp.bfloat16)
    offset_col = jnp.sum(
        jnp.where(eye, offset_r[...].astype(jnp.float32), 0.0), axis=1, keepdims=True
    ).astype(jnp.int32)
    offset_all = jnp.broadcast_to(offset_col, (senders, 128))

    def fill_pick():
        slot_eye = iota((slots, slots), 0) == iota((slots, slots), 1)
        target_col = jnp.sum(
            jnp.where(slot_eye, target_r[...].astype(jnp.float32), 0.0), axis=1, keepdims=True
        )
        slot_k = iota((slots, slots), 1)
        wanted = jnp.where(slot_k < devices, slot_k * CAP, (slot_k - devices) * CAP + 1)
        target_row = jnp.sum(
            jnp.where(iota((slots, slots), 0) == wanted, target_col, 0.0), axis=0, keepdims=True
        )
        target3 = jnp.concatenate([target_row, target_row, target_row], axis=1)

        def fill(i, carry):
            ids = (iota((tiles, 3 * slots), 0) + i * tiles).astype(jnp.float32)
            pick[pl.ds(pl.multiple_of(i * tiles, tiles), tiles), :] = jnp.where(
                ids == target3, 1.0, 0.0
            ).astype(jnp.bfloat16)
            return carry

        lax.fori_loop(0, planes, fill, 0)

    def fringe_copy(it, k):
        other = lax.rem(me + k, devices)
        start = pl.multiple_of(other * SLOT_ROWS, SLOT_ROWS)
        mine = pl.multiple_of(me * SLOT_ROWS, SLOT_ROWS)
        return pltpu.make_async_remote_copy(
            src_ref=outgoing.at[it, pl.ds(start, NV * CAP), :],
            dst_ref=received.at[it, pl.ds(mine, NV * CAP), :],
            send_sem=fsend.at[it, k],
            recv_sem=frecv.at[it, k],
            device_id=(other // nc, lax.rem(other, nc)),
            device_id_type=MESH,
        )

    def edge_copy(it, side):
        other = lax.rem(c + 1, nc) if side == 0 else lax.rem(c + nc - 1, nc)
        return pltpu.make_async_remote_copy(
            src_ref=edge_out.at[it, side],
            dst_ref=edge_in.at[it, side],
            send_sem=esend.at[it, side],
            recv_sem=erecv.at[it, side],
            device_id=(s, other),
            device_id_type=MESH,
        )

    def member(other_group, across):
        return other_group * 2 + (1 - core if across else core)

    partner = member(group, True)

    def face_copy(it, kind, way, source, target, to):
        return pltpu.make_async_remote_copy(
            src_ref=source,
            dst_ref=target,
            send_sem=csend.at[it, way],
            recv_sem=crecv.at[it, kind],
            device_id=(to, c),
            device_id_type=MESH,
        )

    def mats_copy(k):
        third = pl.ds(k * MATS, MATS)
        return pltpu.make_async_remote_copy(
            src_ref=mats.at[2, third],
            dst_ref=mats.at[core, third],
            send_sem=msend.at[k],
            recv_sem=mrecv.at[k],
            device_id=(partner, c),
            device_id_type=MESH,
        )

    def b_to_partner(it):
        return face_copy(it, 0, 0, zero.at[it, 2, 0], zero.at[it, core, 0], partner)

    def c_to_partner(it):
        return face_copy(it, 1, 1, zero.at[it, 2, 1], zero.at[it, core, 1], partner)

    parts = [pl.ds(k * PART, PART) for k in range(half // PART)]

    def x_to_next(it, k, source):
        rows = parts[k]
        return face_copy(
            it, 2 + k, 2 + k, source.at[it, :, rows, :], x_in.at[it, :, rows, :], member(group + 1, True)
        )

    def y_to_prev(it, k):
        rows = parts[k]
        n = 2 + len(parts) + k
        return face_copy(
            it, n, n, y_out.at[it, :, rows, :], y_in.at[it, :, rows, :], member(group - 1, True)
        )

    own_rows = pl.ds(pl.multiple_of(own_base, half), half)

    def x_to_partner(it):
        source = x_face.at[it, 1 - core, :, own_rows, :]
        n = 2 + 2 * len(parts)
        return face_copy(it, n, n, source, source, partner)

    def y_to_partner(it, k, send):
        side, base = (1 - core, own_base) if send else (core, far_base)
        rows = pl.ds(pl.multiple_of(base + k * PART, PART), PART)
        source = y_face.at[it, side, :, rows, :]
        n = 3 + 2 * len(parts) + k
        return face_copy(it, n, n, source, source, partner)

    def block(rows):
        return [inverse[k, rows, :] for k in range(len(PAIRS))]

    def dot(terms):
        total = None
        for left, right in terms:
            total = left * right if total is None else total + left * right
        return total

    def apply(blocks, vector):
        return [dot([(blocks[pair(a, b)], vector[b]) for b in range(NV)]) for a in range(NV)]

    def at(base, size):
        return pl.ds(pl.multiple_of(base, 8), size)

    def matrix(ref, first, rows):
        return [[ref[first + a * NV + b, rows, :] for b in range(NV)] for a in range(NV)]

    def times(rows_of_matrix, vector):
        return [dot([(rows_of_matrix[a][b], vector[b]) for b in range(NV)]) for a in range(NV)]

    def column(m, b):
        return [m[a][b] for a in range(NV)]

    def send_donors(it):
        for v in range(NV):
            edge_out[it, 0, v] = state[v, pl.ds(tiles - 1, planes, stride=tiles), :]
            edge_out[it, 1, v] = state[v, pl.ds(0, planes, stride=tiles), :]
        for side in range(2):
            edge_copy(it, side).start()

        def gather(q, carry):
            for k in range(8):
                e = q * 8 + k
                chosen = block_s[e]
                for v in range(NV):
                    gathered[v, pl.ds(e, 1), :] = state[v, pl.ds(chosen, 1), :]
            return carry

        lax.fori_loop(0, senders // 8, gather, 0)
        weight = weight_r[...]
        for v in range(NV):
            chosen = gathered[v]
            moved = chosen
            for bit in range(7):
                rolled = pltpu.roll(moved, 128 - (1 << bit), 1)
                moved = jnp.where((offset_all & (1 << bit)) != 0, rolled, moved)
            placed[:, v * 128:(v + 1) * 128] = split3(weight * (chosen + moved))
        slot_values = jnp.dot(place3, placed[...], preferred_element_type=jnp.float32)
        for v in range(NV):
            for k in range(CAP):
                outgoing[it, pl.ds(v * CAP + k, devices, stride=SLOT_ROWS), :] = slot_values[
                    k * devices:(k + 1) * devices, v * 128:(v + 1) * 128
                ]

        def send(k, carry):
            fringe_copy(it, k).start()
            return carry

        lax.fori_loop(1, devices, send, 0)
        mine = pl.ds(pl.multiple_of(me * SLOT_ROWS, SLOT_ROWS), NV * CAP)
        received[it, mine, :] = outgoing[it, mine, :]

    def transfer(q, carry):
        each = half // 8
        local = lax.rem(q, each) * 8
        base = jnp.where(q < each, far_base, own_base) + local
        slot = jnp.where(q < each, 2, core)
        spot = at(local, 8)
        for cols in BATCHES:
            chain = None
            for i in range(planes):
                rows = at(i * tiles + base, 8)
                blocks = block(rows)
                factor = [lower[v, rows, :] for v in range(NV)]
                if i == 0:
                    chain = {b: [blocks[pair(a, b)] * factor[b] for a in range(NV)] for b in cols}
                else:
                    chain = {
                        b: apply(blocks, [factor[v] * chain[b][v] for v in range(NV)]) for b in cols
                    }
                if i < planes - 1:
                    for b in cols:
                        for a in range(NV):
                            stage[i, a * NV + b] = chain[b][a]
            for b in cols:
                for a in range(NV):
                    mats[slot, a * NV + b, spot, :] = chain[b][a]
            both = chain
            for i in reversed(range(planes - 1)):
                rows = at(i * tiles + base, 8)
                blocks = block(rows)
                factor = [upper[v, rows, :] for v in range(NV)]
                both = {
                    b: [
                        stage[i, a * NV + b] + z
                        for a, z in enumerate(
                            apply(blocks, [factor[v] * both[b][v] for v in range(NV)])
                        )
                    ]
                    for b in cols
                }
            for b in cols:
                for a in range(NV):
                    mats[slot, 2 * MATS + a * NV + b, spot, :] = both[b][a]
            back = None
            for i in reversed(range(planes)):
                rows = at(i * tiles + base, 8)
                blocks = block(rows)
                factor = [upper[v, rows, :] for v in range(NV)]
                if i == planes - 1:
                    back = {b: [blocks[pair(a, b)] * factor[b] for a in range(NV)] for b in cols}
                else:
                    back = {
                        b: apply(blocks, [factor[v] * back[b][v] for v in range(NV)]) for b in cols
                    }
            for b in cols:
                for a in range(NV):
                    mats[slot, MATS + a * NV + b, spot, :] = back[b][a]

        @pl.when(q == each - 2)
        def _():
            for copy in state_loads:
                copy.wait()
            pl.semaphore_wait(barrier, devices - 1)
            send_donors(0)

        @pl.when(q == each - 1)
        def _():
            for k in range(3):
                mats_copy(k).start()

        return carry

    def compose(q, carry):
        rows = at(q * 8, 8)
        low_a = matrix(mats.at[0], 0, rows)
        high_a = matrix(mats.at[1], 0, rows)
        for b in range(NV):
            out = times(high_a, column(low_a, b))
            for a in range(NV):
                comp[a * NV + b, rows, :] = out[a]
        low_e = matrix(mats.at[0], MATS, rows)
        high_e = matrix(mats.at[1], MATS, rows)
        for b in range(NV):
            out = times(low_e, column(high_e, b))
            for a in range(NV):
                comp[MATS + a * NV + b, rows, :] = out[a]
        high_d = matrix(mats.at[1], 2 * MATS, rows)
        for b in range(NV):
            inner = times(high_d, column(low_a, b))
            out = times(low_e, inner)
            for a in range(NV):
                k = 2 * MATS + a * NV + b
                comp[k, rows, :] = mats[0, k, rows, :] + out[a]
        return carry

    def zero_down(it, base, slot):
        for g in range(half // STEP):
            x = None
            for i in range(planes):
                rows = at(i * tiles + base + g * STEP, STEP)
                t = [drive[v, rows, :] for v in range(NV)]
                if x is not None:
                    t = [t[v] + lower[v, rows, :] * x[v] for v in range(NV)]
                x = apply(block(rows), t)
                for v in range(NV):
                    near[v, rows, :] = x[v]
            for v in range(NV):
                zero[it, slot, 0, v, pl.ds(g * STEP, STEP), :] = x[v]

    def zero_up(it, base, slot):
        for g in range(half // STEP):
            rows = at((planes - 1) * tiles + base + g * STEP, STEP)
            y = [near[v, rows, :] for v in range(NV)]
            for i in reversed(range(planes - 1)):
                rows = at(i * tiles + base + g * STEP, STEP)
                z = apply(block(rows), [upper[v, rows, :] * y[v] for v in range(NV)])
                y = [near[v, rows, :] + z[v] for v in range(NV)]
            for v in range(NV):
                zero[it, slot, 1, v, pl.ds(g * STEP, STEP), :] = y[v]

    def true_down(it, base):
        for g in range(half // STEP):
            x = [x_face[it, core, v, at(base + g * STEP, STEP), :] for v in range(NV)]
            for i in range(planes):
                rows = at(i * tiles + base + g * STEP, STEP)
                t = [drive[v, rows, :] + lower[v, rows, :] * x[v] for v in range(NV)]
                x = apply(block(rows), t)
                for v in range(NV):
                    near[v, rows, :] = x[v]

    def true_up(it, base):
        for g in range(half // STEP):
            y = [y_face[it, core, v, at(base + g * STEP, STEP), :] for v in range(NV)]
            for i in reversed(range(planes)):
                rows = at(i * tiles + base + g * STEP, STEP)
                z = apply(block(rows), [upper[v, rows, :] * y[v] for v in range(NV)])
                y = [near[v, rows, :] + z[v] for v in range(NV)]
                for v in range(NV):
                    if it == ITERS - 1:
                        update[v, rows, :] = y[v]
                    state[v, rows, :] = state[v, rows, :] + y[v]

    def out_copies(part, base):
        copies = []
        for i in range(planes):
            rows = pl.ds(pl.multiple_of(i * tiles + base, half), half)
            cells = pl.ds(pl.multiple_of(base, half), half)
            for n, (source, target) in enumerate(((state, final_h), (update, update_h))):
                copies.append(
                    pltpu.make_async_copy(
                        source.at[:, rows, :], target.at[:, cells, i, :], out_sem.at[part, i, n]
                    )
                )
        return copies

    steps = [pl.ds(g * STEP, STEP) for g in range(half // STEP)]

    def chip_forward(it):
        for rows in steps:
            low = [zero[it, 0, 0, v, rows, :] for v in range(NV)]
            out = times(matrix(mats.at[1], 0, rows), low)
            for v in range(NV):
                chip_b[it, v, rows, :] = zero[it, 1, 0, v, rows, :] + out[v]

    def chip_backward(it):
        for rows in steps:
            low = [zero[it, 0, 0, v, rows, :] for v in range(NV)]
            out = times(matrix(mats.at[1], 2 * MATS, rows), low)
            out = [out[v] + zero[it, 1, 1, v, rows, :] for v in range(NV)]
            out = times(matrix(mats.at[0], MATS, rows), out)
            for v in range(NV):
                chip_c[it, v, rows, :] = zero[it, 0, 1, v, rows, :] + out[v]

    def own(g):
        return at(own_base + g * STEP, STEP)

    def relay_forward(it):
        for k, rows in enumerate(parts):
            @pl.when(jnp.logical_not(first))
            def _():
                x_to_next(it, k, x_out).wait_recv()

            x = [x_in[it, v, rows, :] for v in range(NV)]
            out = times(matrix(comp, 0, rows), x)
            for v in range(NV):
                x_out[it, v, rows, :] = chip_b[it, v, rows, :] + out[v]
                x_face[it, 0, v, at(own_base + k * PART, PART), :] = x[v]

            @pl.when(jnp.logical_not(first | last))
            def _():
                x_to_next(it, k, x_out).start()

    def turn(it):
        for g, rows in enumerate(steps):
            x = [x_face[it, 0, v, own(g), :] for v in range(NV)]
            out = times(matrix(comp, 2 * MATS, rows), x)
            for v in range(NV):
                g_own[it, v, rows, :] = chip_c[it, v, rows, :] + out[v]

    def inner_forward(it):
        for g, rows in enumerate(steps):
            x = [x_face[it, 0, v, own(g), :] for v in range(NV)]
            out = times(matrix(mats.at[0], 0, rows), x)
            high = [zero[it, 0, 0, v, rows, :] + out[v] for v in range(NV)]
            out = times(matrix(mats.at[1], 2 * MATS, rows), high)
            for v in range(NV):
                x_face[it, 1, v, own(g), :] = high[v]
                g_inner[it, v, rows, :] = zero[it, 1, 1, v, rows, :] + out[v]

    def relay_backward(it):
        for k, rows in enumerate(parts):
            @pl.when(jnp.logical_not(last))
            def _():
                y_to_prev(it, k).wait_recv()

            y = [y_in[it, v, rows, :] for v in range(NV)]
            out = times(matrix(comp, MATS, rows), y)
            for v in range(NV):
                y_out[it, v, rows, :] = g_own[it, v, rows, :] + out[v]

            @pl.when(jnp.logical_not(first))
            def _():
                y_to_prev(it, k).start()

            mine = at(own_base + k * PART, PART)
            back = times(matrix(mats.at[1], MATS, rows), y)
            for v in range(NV):
                y_face[it, 1, v, mine, :] = y[v]
                y_face[it, 0, v, mine, :] = g_inner[it, v, rows, :] + back[v]
            y_to_partner(it, k, True).start()

    face_zero = jnp.zeros((NV, half, 128), jnp.float32)

    @pl.when(first)
    def _():
        for it in range(ITERS):
            x_in[it] = face_zero

    @pl.when(last)
    def _():
        for it in range(ITERS):
            y_in[it] = face_zero

    for it in range(ITERS):
        if it > 0:
            send_donors(it)
        if it == 0:
            fill_pick()
            for copy in sweep_loads:
                copy.wait()
            lax.fori_loop(0, tiles // 8, transfer, 0)
            for copy in drive_loads:
                copy.wait()
        lane = iota((tiles, 128), 1)
        row = iota((tiles, 128), 0)

        def drive_plane(i, carry):
            rows = pl.ds(pl.multiple_of(i * tiles, tiles), tiles)
            factor = coupling[rows, :]
            for v in range(NV):
                x = state[v, rows, :]
                left = pltpu.roll(x, 1, 1)
                left = jnp.where(
                    lane == 0, jnp.where(row == 0, 0.0, pltpu.roll(left, 1, 0)), left
                )
                right = pltpu.roll(x, 127, 1)
                right = jnp.where(
                    lane == 127,
                    jnp.where(row == tiles - 1, 0.0, pltpu.roll(right, tiles - 1, 0)),
                    right,
                )
                drive[v, rows, :] = forcing[v, rows, :] - factor * (2.0 * x - left - right)
            return carry

        lax.fori_loop(0, planes, drive_plane, 0)
        for side in range(2):
            edge_copy(it, side).wait_recv()
            rows = pl.ds(0 if side == 0 else tiles - 1, planes, stride=tiles)
            hit = iota((planes, 128), 1) == (0 if side == 0 else 127)
            for v in range(NV):
                beyond = pltpu.roll(edge_in[it, side, v], 1 if side == 0 else 127, 1)
                drive[v, rows, :] = drive[v, rows, :] + coupling[rows, :] * jnp.where(
                    hit, beyond, 0.0
                )

        def take(k, carry):
            fringe_copy(it, k).wait_recv()
            return carry

        lax.fori_loop(1, devices, take, 0)
        for v in range(NV):
            pieces = [
                received[it, pl.ds(v * CAP + k, devices, stride=SLOT_ROWS), :] for k in range(CAP)
            ]
            stacked[:, v * 128:(v + 1) * 128] = split3(jnp.concatenate(pieces, axis=0))

        def add_fringe(i, carry):
            rows = pl.ds(pl.multiple_of(i * tiles, tiles), tiles)
            hole = (1 - blank[rows, :]).astype(jnp.float32)
            fringe = jnp.dot(pick[rows, :], stacked[...], preferred_element_type=jnp.float32)
            for v in range(NV):
                drive[v, rows, :] = drive[v, rows, :] + hole * fringe[:, v * 128:(v + 1) * 128]
            return carry

        lax.fori_loop(0, planes, add_fringe, 0, unroll=True)

        zero_down(it, far_base, 2)
        b_to_partner(it).start()
        zero_down(it, own_base, core)
        if it == 0:
            for k in range(3):
                mats_copy(k).wait_recv()
        b_to_partner(it).wait_recv()
        chip_forward(it)

        @pl.when(first)
        def _():
            for k in range(len(parts)):
                x_to_next(it, k, chip_b).start()

        zero_up(it, far_base, 2)
        c_to_partner(it).start()
        zero_up(it, own_base, core)
        if it == 0:
            lax.fori_loop(0, half // 8, compose, 0)
        c_to_partner(it).wait_recv()
        chip_backward(it)
        relay_forward(it)
        turn(it)
        inner_forward(it)

        @pl.when(last)
        def _():
            relay_backward(it)

        x_to_partner(it).start()
        true_down(it, own_base)
        x_to_partner(it).wait_recv()
        true_down(it, far_base)

        @pl.when(jnp.logical_not(last))
        def _():
            relay_backward(it)

        true_up(it, own_base)
        if it == ITERS - 1:
            for copy in out_copies(0, own_base):
                copy.start()
        for k in range(len(parts)):
            y_to_partner(it, k, False).wait_recv()
        true_up(it, far_base)
        if it == ITERS - 1:
            for copy in out_copies(1, far_base):
                copy.start()

    for k in range(3):
        mats_copy(k).wait_send()

    for it in range(ITERS):
        for side in range(2):
            edge_copy(it, side).wait_send()

        def sent(k, carry):
            fringe_copy(it, k).wait_send()
            return carry

        lax.fori_loop(1, devices, sent, 0)
        b_to_partner(it).wait_send()
        c_to_partner(it).wait_send()
        x_to_partner(it).wait_send()
        for k in range(len(parts)):
            y_to_partner(it, k, True).wait_send()

        @pl.when(jnp.logical_not(last))
        def _():
            for k in range(len(parts)):
                x_to_next(it, k, x_out).wait_send()

        @pl.when(jnp.logical_not(first))
        def _():
            for k in range(len(parts)):
                y_to_prev(it, k).wait_send()

    for part, base in enumerate((own_base, far_base)):
        for copy in out_copies(part, base):
            copy.wait()


def shards(
    initial_state, forcing, block_inverse, lower_decay, upper_decay, cross_coupling, iblank,
    donor_receiver, donor_block, stencil_offset, stencil_weight, fringe_target,
):
    ns, nc = lax.axis_size("stream"), lax.axis_size("cross")
    devices = ns * nc
    planes, cells = initial_state.shape[1:]
    tiles = cells // 128
    senders = donor_block.shape[0]
    slots = devices * CAP

    def tiled(x):
        lead = x.shape[:-2]
        n = len(lead)
        order = tuple(range(n)) + (n + 1, n, n + 2)
        return x.reshape(lead + (planes, tiles, 128)).transpose(order)

    def untiled(x):
        return x.transpose(0, 2, 1, 3).reshape(NV, planes, cells)

    full = (NV, planes * tiles, 128)
    half = tiles // 2
    f32, bf16 = jnp.float32, jnp.bfloat16
    dma = pltpu.SemaphoreType.DMA
    face = pltpu.VMEM((ITERS, NV, half, 128), f32)
    out = jax.ShapeDtypeStruct((NV, tiles, planes, 128), f32)
    hbm = pl.BlockSpec(memory_space=pl.ANY)
    vmem = pl.BlockSpec(memory_space=pltpu.VMEM)
    smem = pl.BlockSpec(memory_space=pltpu.SMEM)
    final, update = pl.pallas_call(
        functools.partial(kernel, ns, nc, planes, tiles),
        out_shape=(out, out),
        in_specs=[hbm] * 7 + [vmem, smem, vmem, vmem, vmem],
        out_specs=(hbm, hbm),
        scratch_shapes=[
            pltpu.VMEM(full, f32),
            pltpu.VMEM(full, f32),
            pltpu.VMEM((len(PAIRS),) + full[1:], f32),
            pltpu.VMEM(full, f32),
            pltpu.VMEM(full, f32),
            pltpu.VMEM(full[1:], f32),
            pltpu.VMEM(full[1:], jnp.int32),
            pltpu.VMEM(full, f32),
            pltpu.VMEM(full, f32),
            pltpu.VMEM(full, f32),
            pltpu.VMEM((NV, senders, 128), f32),
            pltpu.VMEM((3 * senders, NV * 128), bf16),
            pltpu.VMEM((ITERS, devices * SLOT_ROWS, 128), f32),
            pltpu.VMEM((ITERS, devices * SLOT_ROWS, 128), f32),
            pltpu.VMEM((planes * tiles, 3 * slots), bf16),
            pltpu.VMEM((3 * slots, NV * 128), bf16),
            pltpu.VMEM((ITERS, 2, NV, planes, 128), f32),
            pltpu.VMEM((ITERS, 2, NV, planes, 128), f32),
            pltpu.VMEM((planes, MATS, 8, 128), f32),
            pltpu.VMEM((3, 3 * MATS, half, 128), f32),
            pltpu.VMEM((3 * MATS, half, 128), f32),
            pltpu.VMEM((ITERS, 3, 2, NV, half, 128), f32),
            face,
            face,
            face,
            face,
            pltpu.VMEM((ITERS, 2, NV, tiles, 128), f32),
            face,
            face,
            face,
            face,
            pltpu.VMEM((ITERS, 2, NV, tiles, 128), f32),
            dma((planes * (4 + 2 + NV),)),
            dma((2, planes, 2)),
            dma((ITERS, devices)),
            dma((ITERS, devices)),
            dma((ITERS, 2)),
            dma((ITERS, 2)),
            dma((3,)),
            dma((3,)),
            dma((ITERS, 3 + 3 * (half // PART))),
            dma((ITERS, 3 + 3 * (half // PART))),
        ],
        compiler_params=pltpu.CompilerParams(
            collective_id=0, has_side_effects=True, vmem_limit_bytes=56 * 1024 * 1024
        ),
    )(
        tiled(initial_state), tiled(forcing), tiled(block_inverse), tiled(lower_decay),
        tiled(upper_decay), tiled(cross_coupling), tiled(iblank),
        donor_receiver.reshape(1, senders), donor_block, stencil_offset.reshape(1, senders), stencil_weight,
        fringe_target.reshape(1, slots),
    )
    return untiled(final), untiled(update)


def solution(mesh):
    return jax.shard_map(
        shards,
        mesh=mesh,
        in_specs=(
            P(None, "stream", "cross"),
            P(None, "stream", "cross"),
            P(None, None, "stream", "cross"),
            P(None, "stream", "cross"),
            P(None, "stream", "cross"),
            P("stream", "cross"),
            P("stream", "cross"),
            P(("stream", "cross"), None),
            P(("stream", "cross")),
            P(("stream", "cross")),
            P(("stream", "cross"), None),
            P(("stream", "cross")),
        ),
        out_specs=(P(None, "stream", "cross"), P(None, "stream", "cross")),
        check_vma=False,
    )
```

```python
import functools

import jax
import jax.numpy as jnp
from jax import lax
from jax.experimental import pallas as pl
from jax.experimental.pallas import tpu as pltpu
from jax.sharding import PartitionSpec as P

ITERS = 2
CAP = 2
NV = 5
SLOT_ROWS = 16
STEP = 16
PART = 8
MATS = NV * NV
PIECES = ((0, 13), (13, 12))
BATCHES = ((0, 1, 2, 3, 4),)
MESH = pl.DeviceIdType.MESH
PAIRS = [(a, b) for a in range(NV) for b in range(a, NV)]


def pair(a, b):
    return PAIRS.index((min(a, b), max(a, b)))


def split3(x):
    high = x.astype(jnp.bfloat16)
    rest = x - high.astype(jnp.float32)
    mid = rest.astype(jnp.bfloat16)
    low = (rest - mid.astype(jnp.float32)).astype(jnp.bfloat16)
    return jnp.concatenate([high, mid, low], axis=0)


def iota(shape, dim):
    return lax.broadcasted_iota(jnp.int32, shape, dim)


def kernel(
    ns, nc, planes, tiles,
    state_h, forcing_h, inverse_h, lower_h, upper_h, coupling_h, blank_h,
    receiver_r, block_s, offset_r, weight_r, target_r,
    final_h, update_h,
    state, forcing, inverse, lower, upper, coupling, blank,
    drive, near, update, gathered, placed, outgoing, received, pick, stacked,
    edge_out, edge_in,
    stage, mats, comp, all_m, all_b, all_g,
    zero, chip_b, chip_c, x_in, x_out, x_face, g_own, g_inner, y_in, y_out, y_face,
    load_sem, out_sem, fsend, frecv, esend, erecv, msend, mrecv, csend, crecv,
    asend, arecv, dsend, drecv,
):
    s, c = lax.axis_index("stream"), lax.axis_index("cross")
    devices = ns * nc
    me = s * nc + c
    senders = block_s.shape[0]
    slots = devices * CAP
    groups = ns // 2
    half = tiles // 2
    core = lax.rem(s, 2)
    group = s // 2
    first, last = group == 0, group == groups - 1
    even = lax.rem(group, 2) == 0
    own_base = lax.rem(core + group, 2) * half
    far_base = half - own_base

    loads = []

    def load(source, target):
        copy = pltpu.make_async_copy(source, target, load_sem.at[len(loads)])
        copy.start()
        loads.append(copy)
        return copy

    def rows_of(i):
        return pl.ds(i * tiles, tiles)

    sweep_loads = []
    for i in range(planes):
        sweep_loads.append(load(lower_h.at[:, :, i, :], lower.at[:, rows_of(i), :]))
        for a in range(NV):
            top = pair(a, a)
            sweep_loads.append(
                load(
                    inverse_h.at[a, pl.ds(a, NV - a), :, i, :],
                    inverse.at[pl.ds(top, NV - a), rows_of(i), :],
                )
            )
    for i in range(planes):
        sweep_loads.append(load(upper_h.at[:, :, i, :], upper.at[:, rows_of(i), :]))
    barrier = pltpu.get_barrier_semaphore()

    def greet(k, carry):
        other = lax.rem(me + k, devices)
        pl.semaphore_signal(
            barrier, inc=1, device_id=(other // nc, lax.rem(other, nc)), device_id_type=MESH
        )
        return carry

    lax.fori_loop(1, devices, greet, 0)

    state_loads = [load(state_h.at[:, :, i, :], state.at[:, rows_of(i), :]) for i in range(planes)]
    drive_loads = []
    for i in range(planes):
        drive_loads.append(load(forcing_h.at[:, :, i, :], forcing.at[:, rows_of(i), :]))
        drive_loads.append(load(coupling_h.at[:, i, :], coupling.at[rows_of(i), :]))
        drive_loads.append(load(blank_h.at[:, i, :], blank.at[rows_of(i), :]))

    eye = iota((senders, senders), 0) == iota((senders, senders), 1)
    recv_row = receiver_r[...].astype(jnp.float32)
    recv_col = jnp.sum(jnp.where(eye, recv_row, 0.0), axis=1, keepdims=True)
    earlier = iota((senders, senders), 0) < iota((senders, senders), 1)
    rank_row = jnp.sum(
        jnp.where(earlier & (recv_col == recv_row), 1.0, 0.0), axis=0, keepdims=True
    )
    key_row = rank_row * devices + recv_row
    place = (key_row == iota((slots, senders), 0).astype(jnp.float32)).astype(jnp.float32)
    place3 = jnp.concatenate([place, place, place], axis=1).astype(jnp.bfloat16)
    offset_col = jnp.sum(
        jnp.where(eye, offset_r[...].astype(jnp.float32), 0.0), axis=1, keepdims=True
    ).astype(jnp.int32)
    offset_all = jnp.broadcast_to(offset_col, (senders, 128))

    def fill_pick():
        slot_eye = iota((slots, slots), 0) == iota((slots, slots), 1)
        target_col = jnp.sum(
            jnp.where(slot_eye, target_r[...].astype(jnp.float32), 0.0), axis=1, keepdims=True
        )
        slot_k = iota((slots, slots), 1)
        wanted = jnp.where(slot_k < devices, slot_k * CAP, (slot_k - devices) * CAP + 1)
        target_row = jnp.sum(
            jnp.where(iota((slots, slots), 0) == wanted, target_col, 0.0), axis=0, keepdims=True
        )
        target3 = jnp.concatenate([target_row, target_row, target_row], axis=1)

        def fill(i, carry):
            ids = (iota((tiles, 3 * slots), 0) + i * tiles).astype(jnp.float32)
            pick[pl.ds(pl.multiple_of(i * tiles, tiles), tiles), :] = jnp.where(
                ids == target3, 1.0, 0.0
            ).astype(jnp.bfloat16)
            return carry

        lax.fori_loop(0, planes, fill, 0)

    def fringe_copy(it, k):
        other = lax.rem(me + k, devices)
        start = pl.multiple_of(other * SLOT_ROWS, SLOT_ROWS)
        mine = pl.multiple_of(me * SLOT_ROWS, SLOT_ROWS)
        return pltpu.make_async_remote_copy(
            src_ref=outgoing.at[it, pl.ds(start, NV * CAP), :],
            dst_ref=received.at[it, pl.ds(mine, NV * CAP), :],
            send_sem=fsend.at[it, k],
            recv_sem=frecv.at[it, k],
            device_id=(other // nc, lax.rem(other, nc)),
            device_id_type=MESH,
        )

    def edge_copy(it, side):
        other = lax.rem(c + 1, nc) if side == 0 else lax.rem(c + nc - 1, nc)
        return pltpu.make_async_remote_copy(
            src_ref=edge_out.at[it, side],
            dst_ref=edge_in.at[it, side],
            send_sem=esend.at[it, side],
            recv_sem=erecv.at[it, side],
            device_id=(s, other),
            device_id_type=MESH,
        )

    def member(other_group, across):
        return other_group * 2 + (1 - core if across else core)

    partner = member(group, True)

    def face_copy(it, kind, way, source, target, to):
        return pltpu.make_async_remote_copy(
            src_ref=source,
            dst_ref=target,
            send_sem=csend.at[it, way],
            recv_sem=crecv.at[it, kind],
            device_id=(to, c),
            device_id_type=MESH,
        )

    def mats_copy(k):
        third = pl.ds(k * MATS, MATS)
        return pltpu.make_async_remote_copy(
            src_ref=mats.at[2, third],
            dst_ref=mats.at[core, third],
            send_sem=msend.at[k],
            recv_sem=mrecv.at[k],
            device_id=(partner, c),
            device_id_type=MESH,
        )

    def chip_copy(kind, piece, sender, d):
        first_row, size = piece
        away = d if kind == 0 else -d
        return pltpu.make_async_remote_copy(
            src_ref=comp.at[pl.ds(kind * MATS + first_row, size)],
            dst_ref=all_m.at[kind, sender, pl.ds(first_row, size)],
            send_sem=asend.at[kind, PIECES.index(piece), d],
            recv_sem=arecv.at[kind, PIECES.index(piece), sender],
            device_id=(member(group + away, d % 2 == 1), c),
            device_id_type=MESH,
        )

    def chip_to(kind, d):
        inside = (group > 0) & (group < groups - 1)
        return inside & ((group + d < groups) if kind == 0 else (group >= d))

    def pass_copy(kind, piece, owner):
        rows = pl.ds(piece[0], piece[1])
        source = all_m.at[kind, owner, rows]
        return pltpu.make_async_remote_copy(
            src_ref=source,
            dst_ref=source,
            send_sem=asend.at[kind, PIECES.index(piece), 0],
            recv_sem=arecv.at[kind, PIECES.index(piece), owner],
            device_id=(member(group + (1 if kind else -1), True), c),
            device_id_type=MESH,
        )

    def passes(kind):
        return (even & (group < groups - 2)) if kind else (jnp.logical_not(even) & (group > 1))

    def wait_chip(kind, owner):
        for piece in PIECES:
            chip_copy(kind, piece, owner, 1).wait_recv()

    def wait_mats(kind):
        end = first if kind else last
        for i in range(1, groups - 1):
            due = (group < i) if kind else (group > i)
            passed = passes(kind) & (group == (i - 2 if kind else i + 2)) & jnp.logical_not(end)

            @pl.when(due & jnp.logical_not(passed))
            def _():
                wait_chip(kind, i)

    def pass_on(kind):
        end = first if kind else last
        owner = group + (2 if kind else -2)

        @pl.when(passes(kind))
        def _():
            @pl.when(jnp.logical_not(end))
            def _():
                wait_chip(kind, owner)

            for piece in PIECES:
                pass_copy(kind, piece, owner).start()

    def send_chip(kind, d, pieces, extra):
        @pl.when(chip_to(kind, d) & extra)
        def _():
            for piece in pieces:
                chip_copy(kind, piece, group, d).start()

    def direct_copy(it, kind, sender, d):
        source, target = ((chip_b, all_b), (g_own, all_g))[kind]
        away = d if kind == 0 else -d
        return pltpu.make_async_remote_copy(
            src_ref=source.at[it],
            dst_ref=target.at[it, sender],
            send_sem=dsend.at[it, kind, d],
            recv_sem=drecv.at[it, kind, sender],
            device_id=(member(group + away, d % 2 == 1), c),
            device_id_type=MESH,
        )

    def direct_to(it, kind, d):
        if it == 0:
            return (group + d == groups - 1) if kind == 0 else (group == d)
        return (group + d < groups) if kind == 0 else (group >= d)

    def send_direct(it, kind):
        for d in reversed(range(1, groups)):
            @pl.when(direct_to(it, kind, d))
            def _():
                direct_copy(it, kind, group, d).start()

    def b_to_partner(it):
        return face_copy(it, 0, 0, zero.at[it, 2, 0], zero.at[it, core, 0], partner)

    def c_to_partner(it):
        return face_copy(it, 1, 1, zero.at[it, 2, 1], zero.at[it, core, 1], partner)

    parts = [pl.ds(k * PART, PART) for k in range(half // PART)]

    def x_to_next(it, k, source):
        rows = parts[k]
        return face_copy(
            it, 2 + k, 2 + k, source.at[it, :, rows, :], x_in.at[it, :, rows, :], member(group + 1, True)
        )

    def y_to_prev(it, k):
        rows = parts[k]
        n = 2 + len(parts) + k
        return face_copy(
            it, n, n, y_out.at[it, :, rows, :], y_in.at[it, :, rows, :], member(group - 1, True)
        )

    own_rows = pl.ds(pl.multiple_of(own_base, half), half)

    def x_to_partner(it):
        source = x_face.at[it, 1 - core, :, own_rows, :]
        n = 2 + 2 * len(parts)
        return face_copy(it, n, n, source, source, partner)

    def y_to_partner(it, k, send):
        side, base = (1 - core, own_base) if send else (core, far_base)
        rows = pl.ds(pl.multiple_of(base + k * PART, PART), PART)
        source = y_face.at[it, side, :, rows, :]
        n = 3 + 2 * len(parts) + k
        return face_copy(it, n, n, source, source, partner)

    def block(rows):
        return [inverse[k, rows, :] for k in range(len(PAIRS))]

    def dot(terms):
        total = None
        for left, right in terms:
            total = left * right if total is None else total + left * right
        return total

    def apply(blocks, vector):
        return [dot([(blocks[pair(a, b)], vector[b]) for b in range(NV)]) for a in range(NV)]

    def at(base, size):
        return pl.ds(pl.multiple_of(base, 8), size)

    def matrix(ref, first, rows):
        return [[ref[first + a * NV + b, rows, :] for b in range(NV)] for a in range(NV)]

    def times(rows_of_matrix, vector):
        return [dot([(rows_of_matrix[a][b], vector[b]) for b in range(NV)]) for a in range(NV)]

    def column(m, b):
        return [m[a][b] for a in range(NV)]

    def send_donors(it):
        for v in range(NV):
            edge_out[it, 0, v] = state[v, pl.ds(tiles - 1, planes, stride=tiles), :]
            edge_out[it, 1, v] = state[v, pl.ds(0, planes, stride=tiles), :]
        for side in range(2):
            edge_copy(it, side).start()

        def gather(q, carry):
            for k in range(8):
                e = q * 8 + k
                chosen = block_s[e]
                for v in range(NV):
                    gathered[v, pl.ds(e, 1), :] = state[v, pl.ds(chosen, 1), :]
            return carry

        lax.fori_loop(0, senders // 8, gather, 0)
        weight = weight_r[...]
        for v in range(NV):
            chosen = gathered[v]
            moved = chosen
            for bit in range(7):
                rolled = pltpu.roll(moved, 128 - (1 << bit), 1)
                moved = jnp.where((offset_all & (1 << bit)) != 0, rolled, moved)
            placed[:, v * 128:(v + 1) * 128] = split3(weight * (chosen + moved))
        slot_values = jnp.dot(place3, placed[...], preferred_element_type=jnp.float32)
        for v in range(NV):
            for k in range(CAP):
                outgoing[it, pl.ds(v * CAP + k, devices, stride=SLOT_ROWS), :] = slot_values[
                    k * devices:(k + 1) * devices, v * 128:(v + 1) * 128
                ]

        def send(k, carry):
            fringe_copy(it, k).start()
            return carry

        lax.fori_loop(1, devices, send, 0)
        mine = pl.ds(pl.multiple_of(me * SLOT_ROWS, SLOT_ROWS), NV * CAP)
        received[it, mine, :] = outgoing[it, mine, :]

    def transfer(q, carry):
        each = half // 8
        local = lax.rem(q, each) * 8
        base = jnp.where(q < each, far_base, own_base) + local
        slot = jnp.where(q < each, 2, core)
        spot = at(local, 8)
        for cols in BATCHES:
            chain = None
            for i in range(planes):
                rows = at(i * tiles + base, 8)
                blocks = block(rows)
                factor = [lower[v, rows, :] for v in range(NV)]
                if i == 0:
                    chain = {b: [blocks[pair(a, b)] * factor[b] for a in range(NV)] for b in cols}
                else:
                    chain = {
                        b: apply(blocks, [factor[v] * chain[b][v] for v in range(NV)]) for b in cols
                    }
                if i < planes - 1:
                    for b in cols:
                        for a in range(NV):
                            stage[i, a * NV + b] = chain[b][a]
            for b in cols:
                for a in range(NV):
                    mats[slot, a * NV + b, spot, :] = chain[b][a]
            both = chain
            for i in reversed(range(planes - 1)):
                rows = at(i * tiles + base, 8)
                blocks = block(rows)
                factor = [upper[v, rows, :] for v in range(NV)]
                both = {
                    b: [
                        stage[i, a * NV + b] + z
                        for a, z in enumerate(
                            apply(blocks, [factor[v] * both[b][v] for v in range(NV)])
                        )
                    ]
                    for b in cols
                }
            for b in cols:
                for a in range(NV):
                    mats[slot, 2 * MATS + a * NV + b, spot, :] = both[b][a]
            back = None
            for i in reversed(range(planes)):
                rows = at(i * tiles + base, 8)
                blocks = block(rows)
                factor = [upper[v, rows, :] for v in range(NV)]
                if i == planes - 1:
                    back = {b: [blocks[pair(a, b)] * factor[b] for a in range(NV)] for b in cols}
                else:
                    back = {
                        b: apply(blocks, [factor[v] * back[b][v] for v in range(NV)]) for b in cols
                    }
            for b in cols:
                for a in range(NV):
                    mats[slot, MATS + a * NV + b, spot, :] = back[b][a]

        @pl.when(q == each - 2)
        def _():
            for copy in state_loads:
                copy.wait()
            pl.semaphore_wait(barrier, devices - 1)
            send_donors(0)

        @pl.when(q == each - 1)
        def _():
            for k in range(3):
                mats_copy(k).start()

        return carry

    def compose(q, carry):
        rows = at(q * 8, 8)
        low_a = matrix(mats.at[0], 0, rows)
        high_a = matrix(mats.at[1], 0, rows)
        for b in range(NV):
            out = times(high_a, column(low_a, b))
            for a in range(NV):
                comp[a * NV + b, rows, :] = out[a]
        low_e = matrix(mats.at[0], MATS, rows)
        high_e = matrix(mats.at[1], MATS, rows)
        for b in range(NV):
            out = times(low_e, column(high_e, b))
            for a in range(NV):
                comp[MATS + a * NV + b, rows, :] = out[a]
        high_d = matrix(mats.at[1], 2 * MATS, rows)
        for b in range(NV):
            inner = times(high_d, column(low_a, b))
            out = times(low_e, inner)
            for a in range(NV):
                k = 2 * MATS + a * NV + b
                comp[k, rows, :] = mats[0, k, rows, :] + out[a]
        return carry

    def zero_down(it, base, slot):
        for g in range(half // STEP):
            x = None
            for i in range(planes):
                rows = at(i * tiles + base + g * STEP, STEP)
                t = [drive[v, rows, :] for v in range(NV)]
                if x is not None:
                    t = [t[v] + lower[v, rows, :] * x[v] for v in range(NV)]
                x = apply(block(rows), t)
                for v in range(NV):
                    near[v, rows, :] = x[v]
            for v in range(NV):
                zero[it, slot, 0, v, pl.ds(g * STEP, STEP), :] = x[v]

    def zero_up(it, base, slot):
        for g in range(half // STEP):
            rows = at((planes - 1) * tiles + base + g * STEP, STEP)
            y = [near[v, rows, :] for v in range(NV)]
            for i in reversed(range(planes - 1)):
                rows = at(i * tiles + base + g * STEP, STEP)
                z = apply(block(rows), [upper[v, rows, :] * y[v] for v in range(NV)])
                y = [near[v, rows, :] + z[v] for v in range(NV)]
            for v in range(NV):
                zero[it, slot, 1, v, pl.ds(g * STEP, STEP), :] = y[v]

    def true_down(it, base):
        for g in range(half // STEP):
            x = [x_face[it, core, v, at(base + g * STEP, STEP), :] for v in range(NV)]
            for i in range(planes):
                rows = at(i * tiles + base + g * STEP, STEP)
                t = [drive[v, rows, :] + lower[v, rows, :] * x[v] for v in range(NV)]
                x = apply(block(rows), t)
                for v in range(NV):
                    near[v, rows, :] = x[v]

    def true_up(it, base):
        for g in range(half // STEP):
            y = [y_face[it, core, v, at(base + g * STEP, STEP), :] for v in range(NV)]
            for i in reversed(range(planes)):
                rows = at(i * tiles + base + g * STEP, STEP)
                z = apply(block(rows), [upper[v, rows, :] * y[v] for v in range(NV)])
                y = [near[v, rows, :] + z[v] for v in range(NV)]
                for v in range(NV):
                    if it == ITERS - 1:
                        update[v, rows, :] = y[v]
                    state[v, rows, :] = state[v, rows, :] + y[v]

    def out_copies(part, base):
        copies = []
        for i in range(planes):
            rows = pl.ds(pl.multiple_of(i * tiles + base, half), half)
            cells = pl.ds(pl.multiple_of(base, half), half)
            for n, (source, target) in enumerate(((state, final_h), (update, update_h))):
                copies.append(
                    pltpu.make_async_copy(
                        source.at[:, rows, :], target.at[:, cells, i, :], out_sem.at[part, i, n]
                    )
                )
        return copies

    steps = [pl.ds(g * STEP, STEP) for g in range(half // STEP)]

    def chip_forward(it):
        for rows in steps:
            low = [zero[it, 0, 0, v, rows, :] for v in range(NV)]
            out = times(matrix(mats.at[1], 0, rows), low)
            for v in range(NV):
                chip_b[it, v, rows, :] = zero[it, 1, 0, v, rows, :] + out[v]

    def chip_backward(it):
        for rows in steps:
            low = [zero[it, 0, 0, v, rows, :] for v in range(NV)]
            out = times(matrix(mats.at[1], 2 * MATS, rows), low)
            out = [out[v] + zero[it, 1, 1, v, rows, :] for v in range(NV)]
            out = times(matrix(mats.at[0], MATS, rows), out)
            for v in range(NV):
                chip_c[it, v, rows, :] = zero[it, 0, 1, v, rows, :] + out[v]

    def own(g):
        return at(own_base + g * STEP, STEP)

    def relay_forward(it):
        for k, rows in enumerate(parts):
            @pl.when(jnp.logical_not(first))
            def _():
                x_to_next(it, k, x_out).wait_recv()

            x = [x_in[it, v, rows, :] for v in range(NV)]
            out = times(matrix(comp, 0, rows), x)
            for v in range(NV):
                x_out[it, v, rows, :] = chip_b[it, v, rows, :] + out[v]
                x_face[it, 0, v, at(own_base + k * PART, PART), :] = x[v]

            @pl.when((group > 0) & (group < groups - 2))
            def _():
                x_to_next(it, k, x_out).start()

    def turn(it):
        for g, rows in enumerate(steps):
            x = [x_face[it, 0, v, own(g), :] for v in range(NV)]
            out = times(matrix(comp, 2 * MATS, rows), x)
            for v in range(NV):
                g_own[it, v, rows, :] = chip_c[it, v, rows, :] + out[v]

    def inner_forward(it):
        for g, rows in enumerate(steps):
            x = [x_face[it, 0, v, own(g), :] for v in range(NV)]
            out = times(matrix(mats.at[0], 0, rows), x)
            high = [zero[it, 0, 0, v, rows, :] + out[v] for v in range(NV)]
            out = times(matrix(mats.at[1], 2 * MATS, rows), high)
            for v in range(NV):
                x_face[it, 1, v, own(g), :] = high[v]
                g_inner[it, v, rows, :] = zero[it, 1, 1, v, rows, :] + out[v]

    def relay_backward(it):
        for k, rows in enumerate(parts):
            @pl.when(jnp.logical_not(last))
            def _():
                y_to_prev(it, k).wait_recv()

            y = [y_in[it, v, rows, :] for v in range(NV)]
            out = times(matrix(comp, MATS, rows), y)
            for v in range(NV):
                y_out[it, v, rows, :] = g_own[it, v, rows, :] + out[v]

            @pl.when(group > 1)
            def _():
                y_to_prev(it, k).start()

            mine = at(own_base + k * PART, PART)
            back = times(matrix(mats.at[1], MATS, rows), y)
            for v in range(NV):
                y_face[it, 1, v, mine, :] = y[v]
                y_face[it, 0, v, mine, :] = g_inner[it, v, rows, :] + back[v]
            y_to_partner(it, k, True).start()

    def direct_face(it, kind):
        source, face, side = ((all_b, x_face, 0), (all_g, y_face, 1))[kind]
        far = 0 if kind == 0 else groups - 1
        mine = (group > 0) if kind == 0 else (group < groups - 1)

        @pl.when(jnp.logical_not(mine))
        def _():
            face[it, side, :, own_rows, :] = face_zero

        @pl.when(mine)
        def _():
            direct_copy(it, kind, far, 1).wait_recv()
            face[it, side, :, own_rows, :] = source[it, far]

        inner = range(1, groups - 1)
        for i in inner if kind == 0 else reversed(inner):
            @pl.when((group > i) if kind == 0 else (group < i))
            def _():
                direct_copy(it, kind, i, 1).wait_recv()
                for g, rows in enumerate(steps):
                    x = [face[it, side, v, own(g), :] for v in range(NV)]
                    out = times(matrix(all_m.at[kind, i], 0, rows), x)
                    for v in range(NV):
                        face[it, side, v, own(g), :] = source[it, i, v, rows, :] + out[v]

    def direct_backward(it):
        direct_face(it, 1)
        for k, rows in enumerate(parts):
            mine = at(own_base + k * PART, PART)
            y = [y_face[it, 1, v, mine, :] for v in range(NV)]
            back = times(matrix(mats.at[1], MATS, rows), y)
            for v in range(NV):
                y_face[it, 0, v, mine, :] = g_inner[it, v, rows, :] + back[v]
            y_to_partner(it, k, True).start()

    face_zero = jnp.zeros((NV, half, 128), jnp.float32)

    @pl.when(first)
    def _():
        x_in[0] = face_zero

    @pl.when(last)
    def _():
        y_in[0] = face_zero

    for it in range(ITERS):
        if it > 0:
            send_donors(it)
        if it == 0:
            fill_pick()
            for copy in sweep_loads:
                copy.wait()
            lax.fori_loop(0, tiles // 8, transfer, 0)
            for k in range(3):
                mats_copy(k).wait_recv()
            lax.fori_loop(0, half // 8, compose, 0)
            for kind in range(2):
                for d in range(2, groups):
                    send_chip(kind, d, PIECES, True)
            send_chip(0, 1, PIECES, even)
            send_chip(1, 1, PIECES, jnp.logical_not(even))
            for copy in drive_loads:
                copy.wait()
        lane = iota((tiles, 128), 1)
        row = iota((tiles, 128), 0)

        def drive_plane(i, carry):
            rows = pl.ds(pl.multiple_of(i * tiles, tiles), tiles)
            factor = coupling[rows, :]
            for v in range(NV):
                x = state[v, rows, :]
                left = pltpu.roll(x, 1, 1)
                left = jnp.where(
                    lane == 0, jnp.where(row == 0, 0.0, pltpu.roll(left, 1, 0)), left
                )
                right = pltpu.roll(x, 127, 1)
                right = jnp.where(
                    lane == 127,
                    jnp.where(row == tiles - 1, 0.0, pltpu.roll(right, tiles - 1, 0)),
                    right,
                )
                drive[v, rows, :] = forcing[v, rows, :] - factor * (2.0 * x - left - right)
            return carry

        lax.fori_loop(0, planes, drive_plane, 0)
        for side in range(2):
            edge_copy(it, side).wait_recv()
            rows = pl.ds(0 if side == 0 else tiles - 1, planes, stride=tiles)
            hit = iota((planes, 128), 1) == (0 if side == 0 else 127)
            for v in range(NV):
                beyond = pltpu.roll(edge_in[it, side, v], 1 if side == 0 else 127, 1)
                drive[v, rows, :] = drive[v, rows, :] + coupling[rows, :] * jnp.where(
                    hit, beyond, 0.0
                )

        def take(k, carry):
            fringe_copy(it, k).wait_recv()
            return carry

        lax.fori_loop(1, devices, take, 0)
        for v in range(NV):
            pieces = [
                received[it, pl.ds(v * CAP + k, devices, stride=SLOT_ROWS), :] for k in range(CAP)
            ]
            stacked[:, v * 128:(v + 1) * 128] = split3(jnp.concatenate(pieces, axis=0))

        def add_fringe(i, carry):
            rows = pl.ds(pl.multiple_of(i * tiles, tiles), tiles)
            hole = (1 - blank[rows, :]).astype(jnp.float32)
            fringe = jnp.dot(pick[rows, :], stacked[...], preferred_element_type=jnp.float32)
            for v in range(NV):
                drive[v, rows, :] = drive[v, rows, :] + hole * fringe[:, v * 128:(v + 1) * 128]
            return carry

        lax.fori_loop(0, planes, add_fringe, 0, unroll=True)

        zero_down(it, far_base, 2)
        b_to_partner(it).start()
        zero_down(it, own_base, core)
        b_to_partner(it).wait_recv()
        chip_forward(it)

        if it == 0:
            @pl.when(first)
            def _():
                for k in range(len(parts)):
                    x_to_next(it, k, chip_b).start()

        send_direct(it, 0)

        zero_up(it, far_base, 2)
        c_to_partner(it).start()
        zero_up(it, own_base, core)
        c_to_partner(it).wait_recv()
        chip_backward(it)
        if it == 0:
            @pl.when(last)
            def _():
                wait_mats(0)
                direct_face(it, 0)

            @pl.when(jnp.logical_not(last))
            def _():
                relay_forward(it)
        else:
            @pl.when(jnp.logical_not(last))
            def _():
                wait_mats(0)

            direct_face(it, 0)
        turn(it)
        send_direct(it, 1)
        inner_forward(it)
        if it == 0:
            @pl.when(last)
            def _():
                relay_backward(it)

        x_to_partner(it).start()
        true_down(it, own_base)
        x_to_partner(it).wait_recv()
        true_down(it, far_base)
        if it == 0:
            @pl.when(first)
            def _():
                wait_mats(1)

            pass_on(1)

            @pl.when(first)
            def _():
                direct_backward(it)

            @pl.when(jnp.logical_not(first | last))
            def _():
                relay_backward(it)
        else:
            @pl.when(jnp.logical_not(first))
            def _():
                wait_mats(1)

            direct_backward(it)
        true_up(it, own_base)
        if it == ITERS - 1:
            for copy in out_copies(0, own_base):
                copy.start()
        for k in range(len(parts)):
            y_to_partner(it, k, False).wait_recv()
        true_up(it, far_base)
        if it == 0:
            pass_on(0)
        if it == ITERS - 1:
            for copy in out_copies(1, far_base):
                copy.start()

    for kind in range(2):
        @pl.when(passes(kind))
        def _():
            for piece in PIECES:
                pass_copy(kind, piece, group).wait_send()

        for d in range(1, groups):
            near_by = True if d > 1 else (jnp.logical_not(even) if kind else even)

            @pl.when(chip_to(kind, d) & near_by)
            def _():
                for piece in PIECES:
                    chip_copy(kind, piece, group, d).wait_send()

            for it in range(ITERS):
                @pl.when(direct_to(it, kind, d))
                def _():
                    direct_copy(it, kind, group, d).wait_send()

    for k in range(3):
        mats_copy(k).wait_send()

    for it in range(ITERS):
        for side in range(2):
            edge_copy(it, side).wait_send()

        def sent(k, carry):
            fringe_copy(it, k).wait_send()
            return carry

        lax.fori_loop(1, devices, sent, 0)
        b_to_partner(it).wait_send()
        c_to_partner(it).wait_send()
        x_to_partner(it).wait_send()
        for k in range(len(parts)):
            y_to_partner(it, k, True).wait_send()

        if it > 0:
            continue

        @pl.when(group < groups - 2)
        def _():
            for k in range(len(parts)):
                x_to_next(it, k, x_out).wait_send()

        @pl.when(group > 1)
        def _():
            for k in range(len(parts)):
                y_to_prev(it, k).wait_send()

    for part, base in enumerate((own_base, far_base)):
        for copy in out_copies(part, base):
            copy.wait()


def shards(
    initial_state, forcing, block_inverse, lower_decay, upper_decay, cross_coupling, iblank,
    donor_receiver, donor_block, stencil_offset, stencil_weight, fringe_target,
):
    ns, nc = lax.axis_size("stream"), lax.axis_size("cross")
    devices = ns * nc
    planes, cells = initial_state.shape[1:]
    tiles = cells // 128
    senders = donor_block.shape[0]
    slots = devices * CAP

    def tiled(x):
        lead = x.shape[:-2]
        n = len(lead)
        order = tuple(range(n)) + (n + 1, n, n + 2)
        return x.reshape(lead + (planes, tiles, 128)).transpose(order)

    def untiled(x):
        return x.transpose(0, 2, 1, 3).reshape(NV, planes, cells)

    full = (NV, planes * tiles, 128)
    half = tiles // 2
    groups = ns // 2
    f32, bf16 = jnp.float32, jnp.bfloat16
    dma = pltpu.SemaphoreType.DMA
    face = pltpu.VMEM((ITERS, NV, half, 128), f32)
    out = jax.ShapeDtypeStruct((NV, tiles, planes, 128), f32)
    hbm = pl.BlockSpec(memory_space=pl.ANY)
    vmem = pl.BlockSpec(memory_space=pltpu.VMEM)
    smem = pl.BlockSpec(memory_space=pltpu.SMEM)
    final, update = pl.pallas_call(
        functools.partial(kernel, ns, nc, planes, tiles),
        out_shape=(out, out),
        in_specs=[hbm] * 7 + [vmem, smem, vmem, vmem, vmem],
        out_specs=(hbm, hbm),
        scratch_shapes=[
            pltpu.VMEM(full, f32),
            pltpu.VMEM(full, f32),
            pltpu.VMEM((len(PAIRS),) + full[1:], f32),
            pltpu.VMEM(full, f32),
            pltpu.VMEM(full, f32),
            pltpu.VMEM(full[1:], f32),
            pltpu.VMEM(full[1:], jnp.int32),
            pltpu.VMEM(full, f32),
            pltpu.VMEM(full, f32),
            pltpu.VMEM(full, f32),
            pltpu.VMEM((NV, senders, 128), f32),
            pltpu.VMEM((3 * senders, NV * 128), bf16),
            pltpu.VMEM((ITERS, devices * SLOT_ROWS, 128), f32),
            pltpu.VMEM((ITERS, devices * SLOT_ROWS, 128), f32),
            pltpu.VMEM((planes * tiles, 3 * slots), bf16),
            pltpu.VMEM((3 * slots, NV * 128), bf16),
            pltpu.VMEM((ITERS, 2, NV, planes, 128), f32),
            pltpu.VMEM((ITERS, 2, NV, planes, 128), f32),
            pltpu.VMEM((planes, MATS, 8, 128), f32),
            pltpu.VMEM((3, 3 * MATS, half, 128), f32),
            pltpu.VMEM((3 * MATS, half, 128), f32),
            pltpu.VMEM((2, groups, MATS, half, 128), f32),
            pltpu.VMEM((ITERS, groups, NV, half, 128), f32),
            pltpu.VMEM((ITERS, groups, NV, half, 128), f32),
            pltpu.VMEM((ITERS, 3, 2, NV, half, 128), f32),
            face,
            face,
            face,
            face,
            pltpu.VMEM((ITERS, 2, NV, tiles, 128), f32),
            face,
            face,
            face,
            face,
            pltpu.VMEM((ITERS, 2, NV, tiles, 128), f32),
            dma((planes * (4 + 2 + NV),)),
            dma((2, planes, 2)),
            dma((ITERS, devices)),
            dma((ITERS, devices)),
            dma((ITERS, 2)),
            dma((ITERS, 2)),
            dma((3,)),
            dma((3,)),
            dma((ITERS, 3 + 3 * (half // PART))),
            dma((ITERS, 3 + 3 * (half // PART))),
            dma((2, len(PIECES), groups)),
            dma((2, len(PIECES), groups)),
            dma((ITERS, 2, groups)),
            dma((ITERS, 2, groups)),
        ],
        compiler_params=pltpu.CompilerParams(
            collective_id=0, has_side_effects=True, vmem_limit_bytes=56 * 1024 * 1024
        ),
    )(
        tiled(initial_state), tiled(forcing), tiled(block_inverse), tiled(lower_decay),
        tiled(upper_decay), tiled(cross_coupling), tiled(iblank),
        donor_receiver.reshape(1, senders), donor_block, stencil_offset.reshape(1, senders), stencil_weight,
        fringe_target.reshape(1, slots),
    )
    return untiled(final), untiled(update)


def solution(mesh):
    return jax.shard_map(
        shards,
        mesh=mesh,
        in_specs=(
            P(None, "stream", "cross"),
            P(None, "stream", "cross"),
            P(None, None, "stream", "cross"),
            P(None, "stream", "cross"),
            P(None, "stream", "cross"),
            P("stream", "cross"),
            P("stream", "cross"),
            P(("stream", "cross"), None),
            P(("stream", "cross")),
            P(("stream", "cross")),
            P(("stream", "cross"), None),
            P(("stream", "cross")),
        ),
        out_specs=(P(None, "stream", "cross"), P(None, "stream", "cross")),
        check_vma=False,
    )
```

```python
import functools

import jax
import jax.numpy as jnp
from jax import lax
from jax.experimental import pallas as pl
from jax.experimental.pallas import tpu as pltpu
from jax.sharding import PartitionSpec as P

ITERS = 2
CAP = 2
NV = 5
SLOT_ROWS = 16
STEP = 16
PART = 8
MATS = NV * NV
PIECES = ((0, 13), (13, 12))
MESH = pl.DeviceIdType.MESH
PAIRS = [(a, b) for a in range(NV) for b in range(a, NV)]


def pair(a, b):
    return PAIRS.index((min(a, b), max(a, b)))


def split3(x):
    high = x.astype(jnp.bfloat16)
    rest = x - high.astype(jnp.float32)
    mid = rest.astype(jnp.bfloat16)
    low = (rest - mid.astype(jnp.float32)).astype(jnp.bfloat16)
    return jnp.concatenate([high, mid, low], axis=0)


def iota(shape, dim):
    return lax.broadcasted_iota(jnp.int32, shape, dim)


def kernel(
    ns, nc, planes, tiles,
    state_h, forcing_h, inverse_h, lower_h, upper_h, coupling_h, blank_h,
    receiver_r, block_s, offset_r, weight_r, target_r,
    final_h, update_h,
    state, forcing, inverse, lower, upper, coupling, blank,
    drive, near, update, gathered, placed, outgoing, received, pick, stacked,
    edge_out, edge_in,
    stage, mats, comp, all_m, all_b, all_g,
    zero, chip_b, chip_c, x_in, x_out, x_face, g_own, g_inner, y_in, y_out, y_face,
    load_sem, out_sem, fsend, frecv, esend, erecv, msend, mrecv, csend, crecv,
    asend, arecv, dsend, drecv,
):
    s, c = lax.axis_index("stream"), lax.axis_index("cross")
    devices = ns * nc
    me = s * nc + c
    senders = block_s.shape[0]
    slots = devices * CAP
    groups = ns // 2
    half = tiles // 2
    core = lax.rem(s, 2)
    group = s // 2
    first, last = group == 0, group == groups - 1
    even = lax.rem(group, 2) == 0
    own_base = lax.rem(core + group, 2) * half
    far_base = half - own_base

    loads = []

    def load(source, target):
        copy = pltpu.make_async_copy(source, target, load_sem.at[len(loads)])
        copy.start()
        loads.append(copy)
        return copy

    def rows_of(i):
        return pl.ds(i * tiles, tiles)

    sweep_loads = []
    for i in range(planes):
        sweep_loads.append(load(lower_h.at[:, :, i, :], lower.at[:, rows_of(i), :]))
        for a in range(NV):
            top = pair(a, a)
            sweep_loads.append(
                load(
                    inverse_h.at[a, pl.ds(a, NV - a), :, i, :],
                    inverse.at[pl.ds(top, NV - a), rows_of(i), :],
                )
            )
    upper_loads = []
    for i in range(planes):
        upper_loads.append(load(upper_h.at[:, :, i, :], upper.at[:, rows_of(i), :]))
    barrier = pltpu.get_barrier_semaphore()

    def greet(k, carry):
        other = lax.rem(me + k, devices)
        pl.semaphore_signal(
            barrier, inc=1, device_id=(other // nc, lax.rem(other, nc)), device_id_type=MESH
        )
        return carry

    lax.fori_loop(1, devices, greet, 0)

    state_loads = [load(state_h.at[:, :, i, :], state.at[:, rows_of(i), :]) for i in range(planes)]
    drive_loads = []
    for i in range(planes):
        drive_loads.append(load(forcing_h.at[:, :, i, :], forcing.at[:, rows_of(i), :]))
        drive_loads.append(load(coupling_h.at[:, i, :], coupling.at[rows_of(i), :]))
        drive_loads.append(load(blank_h.at[:, i, :], blank.at[rows_of(i), :]))

    eye = iota((senders, senders), 0) == iota((senders, senders), 1)
    recv_row = receiver_r[...].astype(jnp.float32)
    recv_col = jnp.sum(jnp.where(eye, recv_row, 0.0), axis=1, keepdims=True)
    earlier = iota((senders, senders), 0) < iota((senders, senders), 1)
    rank_row = jnp.sum(
        jnp.where(earlier & (recv_col == recv_row), 1.0, 0.0), axis=0, keepdims=True
    )
    key_row = rank_row * devices + recv_row
    place = (key_row == iota((slots, senders), 0).astype(jnp.float32)).astype(jnp.float32)
    place3 = jnp.concatenate([place, place, place], axis=1).astype(jnp.bfloat16)
    offset_col = jnp.sum(
        jnp.where(eye, offset_r[...].astype(jnp.float32), 0.0), axis=1, keepdims=True
    ).astype(jnp.int32)
    offset_all = jnp.broadcast_to(offset_col, (senders, 128))

    def fill_pick():
        slot_eye = iota((slots, slots), 0) == iota((slots, slots), 1)
        target_col = jnp.sum(
            jnp.where(slot_eye, target_r[...].astype(jnp.float32), 0.0), axis=1, keepdims=True
        )
        slot_k = iota((slots, slots), 1)
        wanted = jnp.where(slot_k < devices, slot_k * CAP, (slot_k - devices) * CAP + 1)
        target_row = jnp.sum(
            jnp.where(iota((slots, slots), 0) == wanted, target_col, 0.0), axis=0, keepdims=True
        )
        target3 = jnp.concatenate([target_row, target_row, target_row], axis=1)

        def fill(i, carry):
            ids = (iota((tiles, 3 * slots), 0) + i * tiles).astype(jnp.float32)
            pick[pl.ds(pl.multiple_of(i * tiles, tiles), tiles), :] = jnp.where(
                ids == target3, 1.0, 0.0
            ).astype(jnp.bfloat16)
            return carry

        lax.fori_loop(0, planes, fill, 0)

    def fringe_copy(it, k):
        other = lax.rem(me + k, devices)
        start = pl.multiple_of(other * SLOT_ROWS, SLOT_ROWS)
        mine = pl.multiple_of(me * SLOT_ROWS, SLOT_ROWS)
        return pltpu.make_async_remote_copy(
            src_ref=outgoing.at[it, pl.ds(start, NV * CAP), :],
            dst_ref=received.at[it, pl.ds(mine, NV * CAP), :],
            send_sem=fsend.at[it, k],
            recv_sem=frecv.at[it, k],
            device_id=(other // nc, lax.rem(other, nc)),
            device_id_type=MESH,
        )

    def edge_copy(it, side):
        other = lax.rem(c + 1, nc) if side == 0 else lax.rem(c + nc - 1, nc)
        return pltpu.make_async_remote_copy(
            src_ref=edge_out.at[it, side],
            dst_ref=edge_in.at[it, side],
            send_sem=esend.at[it, side],
            recv_sem=erecv.at[it, side],
            device_id=(s, other),
            device_id_type=MESH,
        )

    def member(other_group, across):
        return other_group * 2 + (1 - core if across else core)

    partner = member(group, True)

    def face_copy(it, kind, way, source, target, to):
        return pltpu.make_async_remote_copy(
            src_ref=source,
            dst_ref=target,
            send_sem=csend.at[it, way],
            recv_sem=crecv.at[it, kind],
            device_id=(to, c),
            device_id_type=MESH,
        )

    def mats_copy(k):
        third = pl.ds(k * MATS, MATS)
        return pltpu.make_async_remote_copy(
            src_ref=mats.at[2, third],
            dst_ref=mats.at[core, third],
            send_sem=msend.at[k],
            recv_sem=mrecv.at[k],
            device_id=(partner, c),
            device_id_type=MESH,
        )

    def chip_copy(kind, piece, sender, d):
        first_row, size = piece
        away = d if kind == 0 else -d
        return pltpu.make_async_remote_copy(
            src_ref=comp.at[pl.ds(kind * MATS + first_row, size)],
            dst_ref=all_m.at[kind, sender, pl.ds(first_row, size)],
            send_sem=asend.at[kind, PIECES.index(piece), d],
            recv_sem=arecv.at[kind, PIECES.index(piece), sender],
            device_id=(member(group + away, d % 2 == 1), c),
            device_id_type=MESH,
        )

    def chip_to(kind, d):
        inside = (group > 0) & (group < groups - 1)
        return inside & ((group + d < groups) if kind == 0 else (group >= d))

    def pass_copy(kind, piece, owner):
        rows = pl.ds(piece[0], piece[1])
        source = all_m.at[kind, owner, rows]
        return pltpu.make_async_remote_copy(
            src_ref=source,
            dst_ref=source,
            send_sem=asend.at[kind, PIECES.index(piece), 0],
            recv_sem=arecv.at[kind, PIECES.index(piece), owner],
            device_id=(member(group + (1 if kind else -1), True), c),
            device_id_type=MESH,
        )

    def passes(kind):
        return (even & (group < groups - 2)) if kind else (jnp.logical_not(even) & (group > 1))

    def wait_chip(kind, owner):
        for piece in PIECES:
            chip_copy(kind, piece, owner, 1).wait_recv()

    def wait_mats(kind):
        end = first if kind else last
        for i in range(1, groups - 1):
            due = (group < i) if kind else (group > i)
            passed = passes(kind) & (group == (i - 2 if kind else i + 2)) & jnp.logical_not(end)

            @pl.when(due & jnp.logical_not(passed))
            def _():
                wait_chip(kind, i)

    def pass_on(kind):
        end = first if kind else last
        owner = group + (2 if kind else -2)

        @pl.when(passes(kind))
        def _():
            @pl.when(jnp.logical_not(end))
            def _():
                wait_chip(kind, owner)

            for piece in PIECES:
                pass_copy(kind, piece, owner).start()

    def send_chip(kind, d, pieces, extra):
        @pl.when(chip_to(kind, d) & extra)
        def _():
            for piece in pieces:
                chip_copy(kind, piece, group, d).start()

    def direct_copy(it, kind, sender, d):
        source, target = ((chip_b, all_b), (g_own, all_g))[kind]
        away = d if kind == 0 else -d
        return pltpu.make_async_remote_copy(
            src_ref=source.at[it],
            dst_ref=target.at[it, sender],
            send_sem=dsend.at[it, kind, d],
            recv_sem=drecv.at[it, kind, sender],
            device_id=(member(group + away, d % 2 == 1), c),
            device_id_type=MESH,
        )

    def direct_to(it, kind, d):
        if it == 0:
            return (group + d == groups - 1) if kind == 0 else (group == d)
        return (group + d < groups) if kind == 0 else (group >= d)

    def send_direct(it, kind):
        for d in reversed(range(1, groups)):
            @pl.when(direct_to(it, kind, d))
            def _():
                direct_copy(it, kind, group, d).start()

    def b_to_partner(it):
        return face_copy(it, 0, 0, zero.at[it, 2, 0], zero.at[it, core, 0], partner)

    def c_to_partner(it):
        return face_copy(it, 1, 1, zero.at[it, 2, 1], zero.at[it, core, 1], partner)

    parts = [pl.ds(k * PART, PART) for k in range(half // PART)]

    def x_to_next(it, k, source):
        rows = parts[k]
        return face_copy(
            it, 2 + k, 2 + k, source.at[it, :, rows, :], x_in.at[it, :, rows, :], member(group + 1, True)
        )

    def y_to_prev(it, k):
        rows = parts[k]
        n = 2 + len(parts) + k
        return face_copy(
            it, n, n, y_out.at[it, :, rows, :], y_in.at[it, :, rows, :], member(group - 1, True)
        )

    own_rows = pl.ds(pl.multiple_of(own_base, half), half)

    def x_to_partner(it):
        source = x_face.at[it, 1 - core, :, own_rows, :]
        n = 2 + 2 * len(parts)
        return face_copy(it, n, n, source, source, partner)

    def y_to_partner(it, k, send):
        side, base = (1 - core, own_base) if send else (core, far_base)
        rows = pl.ds(pl.multiple_of(base + k * PART, PART), PART)
        source = y_face.at[it, side, :, rows, :]
        n = 3 + 2 * len(parts) + k
        return face_copy(it, n, n, source, source, partner)

    def block(rows):
        return [inverse[k, rows, :] for k in range(len(PAIRS))]

    def dot(terms):
        total = None
        for left, right in terms:
            total = left * right if total is None else total + left * right
        return total

    def apply(blocks, vector):
        return [dot([(blocks[pair(a, b)], vector[b]) for b in range(NV)]) for a in range(NV)]

    def at(base, size):
        return pl.ds(pl.multiple_of(base, 8), size)

    def matrix(ref, first, rows):
        return [[ref[first + a * NV + b, rows, :] for b in range(NV)] for a in range(NV)]

    def times(rows_of_matrix, vector):
        return [dot([(rows_of_matrix[a][b], vector[b]) for b in range(NV)]) for a in range(NV)]

    def column(m, b):
        return [m[a][b] for a in range(NV)]

    def send_donors(it):
        for v in range(NV):
            edge_out[it, 0, v] = state[v, pl.ds(tiles - 1, planes, stride=tiles), :]
            edge_out[it, 1, v] = state[v, pl.ds(0, planes, stride=tiles), :]
        for side in range(2):
            edge_copy(it, side).start()

        def gather(q, carry):
            for k in range(8):
                e = q * 8 + k
                chosen = block_s[e]
                for v in range(NV):
                    gathered[v, pl.ds(e, 1), :] = state[v, pl.ds(chosen, 1), :]
            return carry

        lax.fori_loop(0, senders // 8, gather, 0)
        weight = weight_r[...]
        for v in range(NV):
            chosen = gathered[v]
            moved = chosen
            for bit in range(7):
                rolled = pltpu.roll(moved, 128 - (1 << bit), 1)
                moved = jnp.where((offset_all & (1 << bit)) != 0, rolled, moved)
            placed[:, v * 128:(v + 1) * 128] = split3(weight * (chosen + moved))
        slot_values = jnp.dot(place3, placed[...], preferred_element_type=jnp.float32)
        for v in range(NV):
            for k in range(CAP):
                outgoing[it, pl.ds(v * CAP + k, devices, stride=SLOT_ROWS), :] = slot_values[
                    k * devices:(k + 1) * devices, v * 128:(v + 1) * 128
                ]

        def send(k, carry):
            fringe_copy(it, k).start()
            return carry

        lax.fori_loop(1, devices, send, 0)
        mine = pl.ds(pl.multiple_of(me * SLOT_ROWS, SLOT_ROWS), NV * CAP)
        received[it, mine, :] = outgoing[it, mine, :]

    each = half // 8

    def place_of(q):
        local = lax.rem(q, each) * 8
        base = jnp.where(q < each, far_base, own_base) + local
        return base, jnp.where(q < each, 2, core), at(local, 8)

    def keep(k, slot, spot, columns):
        for b in range(NV):
            for a in range(NV):
                mats[slot, k * MATS + a * NV + b, spot, :] = columns[b][a]

    def advance(blocks, factor, columns):
        if columns is None:
            return [[blocks[pair(a, b)] * factor[b] for a in range(NV)] for b in range(NV)]
        return [apply(blocks, [factor[v] * columns[b][v] for v in range(NV)]) for b in range(NV)]

    def transfer_a(q, carry):
        base, slot, spot = place_of(q)
        chain = None
        for i in range(planes):
            rows = at(i * tiles + base, 8)
            chain = advance(block(rows), [lower[v, rows, :] for v in range(NV)], chain)
            for b in range(NV):
                for a in range(NV):
                    stage[i, a * NV + b, at(base, 8), :] = chain[b][a]
        keep(0, slot, spot, chain)
        return carry

    def transfer_e(q, carry):
        base, slot, spot = place_of(q)
        back = None
        for i in reversed(range(planes)):
            rows = at(i * tiles + base, 8)
            back = advance(block(rows), [upper[v, rows, :] for v in range(NV)], back)
        keep(1, slot, spot, back)

        @pl.when(q == each - 1)
        def _():
            mats_copy(1).start()

        return carry

    def transfer_d(q, carry):
        base, slot, spot = place_of(q)
        spot_all = at(base, 8)
        both = [
            [stage[planes - 1, a * NV + b, spot_all, :] for a in range(NV)] for b in range(NV)
        ]
        for i in reversed(range(planes - 1)):
            rows = at(i * tiles + base, 8)
            both = advance(block(rows), [upper[v, rows, :] for v in range(NV)], both)
            both = [
                [stage[i, a * NV + b, spot_all, :] + both[b][a] for a in range(NV)]
                for b in range(NV)
            ]
        keep(2, slot, spot, both)

        @pl.when(q == each - 1)
        def _():
            mats_copy(2).start()

        return carry

    def compose_a(q, carry):
        rows = at(q * 8, 8)
        low_a = matrix(mats.at[0], 0, rows)
        high_a = matrix(mats.at[1], 0, rows)
        for b in range(NV):
            out = times(high_a, column(low_a, b))
            for a in range(NV):
                comp[a * NV + b, rows, :] = out[a]
        return carry

    def compose_e(q, carry):
        rows = at(q * 8, 8)
        low_e = matrix(mats.at[0], MATS, rows)
        high_e = matrix(mats.at[1], MATS, rows)
        for b in range(NV):
            out = times(low_e, column(high_e, b))
            for a in range(NV):
                comp[MATS + a * NV + b, rows, :] = out[a]
        return carry

    def compose_d(q, carry):
        rows = at(q * 8, 8)
        low_a = matrix(mats.at[0], 0, rows)
        low_e = matrix(mats.at[0], MATS, rows)
        high_d = matrix(mats.at[1], 2 * MATS, rows)
        for b in range(NV):
            out = times(low_e, times(high_d, column(low_a, b)))
            for a in range(NV):
                k = 2 * MATS + a * NV + b
                comp[k, rows, :] = mats[0, k, rows, :] + out[a]
        return carry

    def send_matrices(kind):
        for d in range(2, groups):
            send_chip(kind, d, PIECES, True)
        send_chip(kind, 1, PIECES, jnp.logical_not(even) if kind else even)

    def zero_down(it, base, slot):
        for g in range(half // STEP):
            x = None
            for i in range(planes):
                rows = at(i * tiles + base + g * STEP, STEP)
                t = [drive[v, rows, :] for v in range(NV)]
                if x is not None:
                    t = [t[v] + lower[v, rows, :] * x[v] for v in range(NV)]
                x = apply(block(rows), t)
                for v in range(NV):
                    near[v, rows, :] = x[v]
            for v in range(NV):
                zero[it, slot, 0, v, pl.ds(g * STEP, STEP), :] = x[v]

    def zero_up(it, base, slot):
        for g in range(half // STEP):
            rows = at((planes - 1) * tiles + base + g * STEP, STEP)
            y = [near[v, rows, :] for v in range(NV)]
            for i in reversed(range(planes - 1)):
                rows = at(i * tiles + base + g * STEP, STEP)
                z = apply(block(rows), [upper[v, rows, :] * y[v] for v in range(NV)])
                y = [near[v, rows, :] + z[v] for v in range(NV)]
            for v in range(NV):
                zero[it, slot, 1, v, pl.ds(g * STEP, STEP), :] = y[v]

    def true_down(it, base):
        for g in range(half // STEP):
            x = [x_face[it, core, v, at(base + g * STEP, STEP), :] for v in range(NV)]
            for i in range(planes):
                rows = at(i * tiles + base + g * STEP, STEP)
                t = [drive[v, rows, :] + lower[v, rows, :] * x[v] for v in range(NV)]
                x = apply(block(rows), t)
                for v in range(NV):
                    near[v, rows, :] = x[v]

    def true_up(it, base):
        for g in range(half // STEP):
            y = [y_face[it, core, v, at(base + g * STEP, STEP), :] for v in range(NV)]
            for i in reversed(range(planes)):
                rows = at(i * tiles + base + g * STEP, STEP)
                z = apply(block(rows), [upper[v, rows, :] * y[v] for v in range(NV)])
                y = [near[v, rows, :] + z[v] for v in range(NV)]
                for v in range(NV):
                    if it == ITERS - 1:
                        update[v, rows, :] = y[v]
                    state[v, rows, :] = state[v, rows, :] + y[v]

    def out_copies(part, base):
        copies = []
        for i in range(planes):
            rows = pl.ds(pl.multiple_of(i * tiles + base, half), half)
            cells = pl.ds(pl.multiple_of(base, half), half)
            for n, (source, target) in enumerate(((state, final_h), (update, update_h))):
                copies.append(
                    pltpu.make_async_copy(
                        source.at[:, rows, :], target.at[:, cells, i, :], out_sem.at[part, i, n]
                    )
                )
        return copies

    steps = [pl.ds(g * STEP, STEP) for g in range(half // STEP)]

    def chip_forward(it):
        for rows in steps:
            low = [zero[it, 0, 0, v, rows, :] for v in range(NV)]
            out = times(matrix(mats.at[1], 0, rows), low)
            for v in range(NV):
                chip_b[it, v, rows, :] = zero[it, 1, 0, v, rows, :] + out[v]

    def chip_backward(it):
        for rows in steps:
            low = [zero[it, 0, 0, v, rows, :] for v in range(NV)]
            out = times(matrix(mats.at[1], 2 * MATS, rows), low)
            out = [out[v] + zero[it, 1, 1, v, rows, :] for v in range(NV)]
            out = times(matrix(mats.at[0], MATS, rows), out)
            for v in range(NV):
                chip_c[it, v, rows, :] = zero[it, 0, 1, v, rows, :] + out[v]

    def own(g):
        return at(own_base + g * STEP, STEP)

    def relay_forward(it):
        for k, rows in enumerate(parts):
            @pl.when(jnp.logical_not(first))
            def _():
                x_to_next(it, k, x_out).wait_recv()

            x = [x_in[it, v, rows, :] for v in range(NV)]
            out = times(matrix(comp, 0, rows), x)
            for v in range(NV):
                x_out[it, v, rows, :] = chip_b[it, v, rows, :] + out[v]
                x_face[it, 0, v, at(own_base + k * PART, PART), :] = x[v]

            @pl.when((group > 0) & (group < groups - 2))
            def _():
                x_to_next(it, k, x_out).start()

    def turn(it):
        for g, rows in enumerate(steps):
            x = [x_face[it, 0, v, own(g), :] for v in range(NV)]
            out = times(matrix(comp, 2 * MATS, rows), x)
            for v in range(NV):
                g_own[it, v, rows, :] = chip_c[it, v, rows, :] + out[v]

    def inner_forward(it):
        for g, rows in enumerate(steps):
            x = [x_face[it, 0, v, own(g), :] for v in range(NV)]
            out = times(matrix(mats.at[0], 0, rows), x)
            high = [zero[it, 0, 0, v, rows, :] + out[v] for v in range(NV)]
            out = times(matrix(mats.at[1], 2 * MATS, rows), high)
            for v in range(NV):
                x_face[it, 1, v, own(g), :] = high[v]
                g_inner[it, v, rows, :] = zero[it, 1, 1, v, rows, :] + out[v]

    def relay_backward(it):
        for k, rows in enumerate(parts):
            @pl.when(jnp.logical_not(last))
            def _():
                y_to_prev(it, k).wait_recv()

            y = [y_in[it, v, rows, :] for v in range(NV)]
            out = times(matrix(comp, MATS, rows), y)
            for v in range(NV):
                y_out[it, v, rows, :] = g_own[it, v, rows, :] + out[v]

            @pl.when(group > 1)
            def _():
                y_to_prev(it, k).start()

            mine = at(own_base + k * PART, PART)
            back = times(matrix(mats.at[1], MATS, rows), y)
            for v in range(NV):
                y_face[it, 1, v, mine, :] = y[v]
                y_face[it, 0, v, mine, :] = g_inner[it, v, rows, :] + back[v]
            y_to_partner(it, k, True).start()

    def direct_face(it, kind):
        source, face, side = ((all_b, x_face, 0), (all_g, y_face, 1))[kind]
        far = 0 if kind == 0 else groups - 1
        mine = (group > 0) if kind == 0 else (group < groups - 1)

        @pl.when(jnp.logical_not(mine))
        def _():
            face[it, side, :, own_rows, :] = face_zero

        @pl.when(mine)
        def _():
            direct_copy(it, kind, far, 1).wait_recv()
            face[it, side, :, own_rows, :] = source[it, far]

        inner = range(1, groups - 1)
        for i in inner if kind == 0 else reversed(inner):
            @pl.when((group > i) if kind == 0 else (group < i))
            def _():
                direct_copy(it, kind, i, 1).wait_recv()
                for g, rows in enumerate(steps):
                    x = [face[it, side, v, own(g), :] for v in range(NV)]
                    out = times(matrix(all_m.at[kind, i], 0, rows), x)
                    for v in range(NV):
                        face[it, side, v, own(g), :] = source[it, i, v, rows, :] + out[v]

    def direct_backward(it):
        direct_face(it, 1)
        for k, rows in enumerate(parts):
            mine = at(own_base + k * PART, PART)
            y = [y_face[it, 1, v, mine, :] for v in range(NV)]
            back = times(matrix(mats.at[1], MATS, rows), y)
            for v in range(NV):
                y_face[it, 0, v, mine, :] = g_inner[it, v, rows, :] + back[v]
            y_to_partner(it, k, True).start()

    face_zero = jnp.zeros((NV, half, 128), jnp.float32)

    @pl.when(first)
    def _():
        x_in[0] = face_zero

    @pl.when(last)
    def _():
        y_in[0] = face_zero

    for it in range(ITERS):
        if it > 0:
            send_donors(it)
        if it == 0:
            fill_pick()
            for copy in sweep_loads:
                copy.wait()
            lax.fori_loop(0, tiles // 8, transfer_a, 0)
            for copy in state_loads:
                copy.wait()
            pl.semaphore_wait(barrier, devices - 1)
            mats_copy(0).start()
            send_donors(0)
            mats_copy(0).wait_recv()
            lax.fori_loop(0, each, compose_a, 0)
            send_matrices(0)
            for copy in upper_loads:
                copy.wait()
            lax.fori_loop(0, tiles // 8, transfer_e, 0)
            mats_copy(1).wait_recv()
            lax.fori_loop(0, each, compose_e, 0)
            send_matrices(1)
            for copy in drive_loads:
                copy.wait()
        lane = iota((tiles, 128), 1)
        row = iota((tiles, 128), 0)

        def drive_plane(i, carry):
            rows = pl.ds(pl.multiple_of(i * tiles, tiles), tiles)
            factor = coupling[rows, :]
            for v in range(NV):
                x = state[v, rows, :]
                left = pltpu.roll(x, 1, 1)
                left = jnp.where(
                    lane == 0, jnp.where(row == 0, 0.0, pltpu.roll(left, 1, 0)), left
                )
                right = pltpu.roll(x, 127, 1)
                right = jnp.where(
                    lane == 127,
                    jnp.where(row == tiles - 1, 0.0, pltpu.roll(right, tiles - 1, 0)),
                    right,
                )
                drive[v, rows, :] = forcing[v, rows, :] - factor * (2.0 * x - left - right)
            return carry

        lax.fori_loop(0, planes, drive_plane, 0)
        for side in range(2):
            edge_copy(it, side).wait_recv()
            rows = pl.ds(0 if side == 0 else tiles - 1, planes, stride=tiles)
            hit = iota((planes, 128), 1) == (0 if side == 0 else 127)
            for v in range(NV):
                beyond = pltpu.roll(edge_in[it, side, v], 1 if side == 0 else 127, 1)
                drive[v, rows, :] = drive[v, rows, :] + coupling[rows, :] * jnp.where(
                    hit, beyond, 0.0
                )

        def take(k, carry):
            fringe_copy(it, k).wait_recv()
            return carry

        lax.fori_loop(1, devices, take, 0)
        for v in range(NV):
            pieces = [
                received[it, pl.ds(v * CAP + k, devices, stride=SLOT_ROWS), :] for k in range(CAP)
            ]
            stacked[:, v * 128:(v + 1) * 128] = split3(jnp.concatenate(pieces, axis=0))

        def add_fringe(i, carry):
            rows = pl.ds(pl.multiple_of(i * tiles, tiles), tiles)
            hole = (1 - blank[rows, :]).astype(jnp.float32)
            fringe = jnp.dot(pick[rows, :], stacked[...], preferred_element_type=jnp.float32)
            for v in range(NV):
                drive[v, rows, :] = drive[v, rows, :] + hole * fringe[:, v * 128:(v + 1) * 128]
            return carry

        lax.fori_loop(0, planes, add_fringe, 0, unroll=True)

        zero_down(it, far_base, 2)
        b_to_partner(it).start()
        zero_down(it, own_base, core)
        b_to_partner(it).wait_recv()
        chip_forward(it)

        if it == 0:
            @pl.when(first)
            def _():
                for k in range(len(parts)):
                    x_to_next(it, k, chip_b).start()

        send_direct(it, 0)

        zero_up(it, far_base, 2)
        c_to_partner(it).start()
        zero_up(it, own_base, core)
        if it == 0:
            @pl.when((group > 0) & (group < groups - 2))
            def _():
                relay_forward(it)

            lax.fori_loop(0, tiles // 8, transfer_d, 0)
            mats_copy(2).wait_recv()
            lax.fori_loop(0, each, compose_d, 0)
        c_to_partner(it).wait_recv()
        chip_backward(it)
        if it == 0:
            @pl.when(last)
            def _():
                wait_mats(0)
                direct_face(it, 0)

            @pl.when(first | (group == groups - 2))
            def _():
                relay_forward(it)
        else:
            @pl.when(jnp.logical_not(last))
            def _():
                wait_mats(0)

            direct_face(it, 0)
        turn(it)
        send_direct(it, 1)
        inner_forward(it)
        if it == 0:
            @pl.when(last)
            def _():
                relay_backward(it)

        x_to_partner(it).start()
        true_down(it, own_base)
        x_to_partner(it).wait_recv()
        true_down(it, far_base)
        if it == 0:
            @pl.when(first)
            def _():
                wait_mats(1)

            pass_on(1)

            @pl.when(first)
            def _():
                direct_backward(it)

            @pl.when(jnp.logical_not(first | last))
            def _():
                relay_backward(it)
        else:
            @pl.when(jnp.logical_not(first))
            def _():
                wait_mats(1)

            direct_backward(it)
        true_up(it, own_base)
        if it == ITERS - 1:
            for copy in out_copies(0, own_base):
                copy.start()
        for k in range(len(parts)):
            y_to_partner(it, k, False).wait_recv()
        true_up(it, far_base)
        if it == 0:
            pass_on(0)
        if it == ITERS - 1:
            for copy in out_copies(1, far_base):
                copy.start()

    for kind in range(2):
        @pl.when(passes(kind))
        def _():
            for piece in PIECES:
                pass_copy(kind, piece, group).wait_send()

        for d in range(1, groups):
            near_by = True if d > 1 else (jnp.logical_not(even) if kind else even)

            @pl.when(chip_to(kind, d) & near_by)
            def _():
                for piece in PIECES:
                    chip_copy(kind, piece, group, d).wait_send()

            for it in range(ITERS):
                @pl.when(direct_to(it, kind, d))
                def _():
                    direct_copy(it, kind, group, d).wait_send()

    for k in range(3):
        mats_copy(k).wait_send()

    for it in range(ITERS):
        for side in range(2):
            edge_copy(it, side).wait_send()

        def sent(k, carry):
            fringe_copy(it, k).wait_send()
            return carry

        lax.fori_loop(1, devices, sent, 0)
        b_to_partner(it).wait_send()
        c_to_partner(it).wait_send()
        x_to_partner(it).wait_send()
        for k in range(len(parts)):
            y_to_partner(it, k, True).wait_send()

        if it > 0:
            continue

        @pl.when(group < groups - 2)
        def _():
            for k in range(len(parts)):
                x_to_next(it, k, x_out).wait_send()

        @pl.when(group > 1)
        def _():
            for k in range(len(parts)):
                y_to_prev(it, k).wait_send()

    for part, base in enumerate((own_base, far_base)):
        for copy in out_copies(part, base):
            copy.wait()


def shards(
    initial_state, forcing, block_inverse, lower_decay, upper_decay, cross_coupling, iblank,
    donor_receiver, donor_block, stencil_offset, stencil_weight, fringe_target,
):
    ns, nc = lax.axis_size("stream"), lax.axis_size("cross")
    devices = ns * nc
    planes, cells = initial_state.shape[1:]
    tiles = cells // 128
    senders = donor_block.shape[0]
    slots = devices * CAP

    def tiled(x):
        lead = x.shape[:-2]
        n = len(lead)
        order = tuple(range(n)) + (n + 1, n, n + 2)
        return x.reshape(lead + (planes, tiles, 128)).transpose(order)

    def untiled(x):
        return x.transpose(0, 2, 1, 3).reshape(NV, planes, cells)

    full = (NV, planes * tiles, 128)
    half = tiles // 2
    groups = ns // 2
    f32, bf16 = jnp.float32, jnp.bfloat16
    dma = pltpu.SemaphoreType.DMA
    face = pltpu.VMEM((ITERS, NV, half, 128), f32)
    out = jax.ShapeDtypeStruct((NV, tiles, planes, 128), f32)
    hbm = pl.BlockSpec(memory_space=pl.ANY)
    vmem = pl.BlockSpec(memory_space=pltpu.VMEM)
    smem = pl.BlockSpec(memory_space=pltpu.SMEM)
    final, update = pl.pallas_call(
        functools.partial(kernel, ns, nc, planes, tiles),
        out_shape=(out, out),
        in_specs=[hbm] * 7 + [vmem, smem, vmem, vmem, vmem],
        out_specs=(hbm, hbm),
        scratch_shapes=[
            pltpu.VMEM(full, f32),
            pltpu.VMEM(full, f32),
            pltpu.VMEM((len(PAIRS),) + full[1:], f32),
            pltpu.VMEM(full, f32),
            pltpu.VMEM(full, f32),
            pltpu.VMEM(full[1:], f32),
            pltpu.VMEM(full[1:], jnp.int32),
            pltpu.VMEM(full, f32),
            pltpu.VMEM(full, f32),
            pltpu.VMEM(full, f32),
            pltpu.VMEM((NV, senders, 128), f32),
            pltpu.VMEM((3 * senders, NV * 128), bf16),
            pltpu.VMEM((ITERS, devices * SLOT_ROWS, 128), f32),
            pltpu.VMEM((ITERS, devices * SLOT_ROWS, 128), f32),
            pltpu.VMEM((planes * tiles, 3 * slots), bf16),
            pltpu.VMEM((3 * slots, NV * 128), bf16),
            pltpu.VMEM((ITERS, 2, NV, planes, 128), f32),
            pltpu.VMEM((ITERS, 2, NV, planes, 128), f32),
            pltpu.VMEM((planes, MATS, tiles, 128), f32),
            pltpu.VMEM((3, 3 * MATS, half, 128), f32),
            pltpu.VMEM((3 * MATS, half, 128), f32),
            pltpu.VMEM((2, groups, MATS, half, 128), f32),
            pltpu.VMEM((ITERS, groups, NV, half, 128), f32),
            pltpu.VMEM((ITERS, groups, NV, half, 128), f32),
            pltpu.VMEM((ITERS, 3, 2, NV, half, 128), f32),
            face,
            face,
            face,
            face,
            pltpu.VMEM((ITERS, 2, NV, tiles, 128), f32),
            face,
            face,
            face,
            face,
            pltpu.VMEM((ITERS, 2, NV, tiles, 128), f32),
            dma((planes * (4 + 2 + NV),)),
            dma((2, planes, 2)),
            dma((ITERS, devices)),
            dma((ITERS, devices)),
            dma((ITERS, 2)),
            dma((ITERS, 2)),
            dma((3,)),
            dma((3,)),
            dma((ITERS, 3 + 3 * (half // PART))),
            dma((ITERS, 3 + 3 * (half // PART))),
            dma((2, len(PIECES), groups)),
            dma((2, len(PIECES), groups)),
            dma((ITERS, 2, groups)),
            dma((ITERS, 2, groups)),
        ],
        compiler_params=pltpu.CompilerParams(
            collective_id=0, has_side_effects=True, vmem_limit_bytes=56 * 1024 * 1024
        ),
    )(
        tiled(initial_state), tiled(forcing), tiled(block_inverse), tiled(lower_decay),
        tiled(upper_decay), tiled(cross_coupling), tiled(iblank),
        donor_receiver.reshape(1, senders), donor_block, stencil_offset.reshape(1, senders), stencil_weight,
        fringe_target.reshape(1, slots),
    )
    return untiled(final), untiled(update)


def solution(mesh):
    return jax.shard_map(
        shards,
        mesh=mesh,
        in_specs=(
            P(None, "stream", "cross"),
            P(None, "stream", "cross"),
            P(None, None, "stream", "cross"),
            P(None, "stream", "cross"),
            P(None, "stream", "cross"),
            P("stream", "cross"),
            P("stream", "cross"),
            P(("stream", "cross"), None),
            P(("stream", "cross")),
            P(("stream", "cross")),
            P(("stream", "cross"), None),
            P(("stream", "cross")),
        ),
        out_specs=(P(None, "stream", "cross"), P(None, "stream", "cross")),
        check_vma=False,
    )
```

```python
import functools

import jax
import jax.numpy as jnp
from jax import lax
from jax.experimental import pallas as pl
from jax.experimental.pallas import tpu as pltpu
from jax.sharding import PartitionSpec as P

ITERS = 2
CAP = 2
NV = 5
SLOT_ROWS = 16
STEP = 16
PART = 8
MATS = NV * NV
PIECES = ((0, 13), (13, 12))
MESH = pl.DeviceIdType.MESH
PAIRS = [(a, b) for a in range(NV) for b in range(a, NV)]


def pair(a, b):
    return PAIRS.index((min(a, b), max(a, b)))


def split3(x):
    high = x.astype(jnp.bfloat16)
    rest = x - high.astype(jnp.float32)
    mid = rest.astype(jnp.bfloat16)
    low = (rest - mid.astype(jnp.float32)).astype(jnp.bfloat16)
    return jnp.concatenate([high, mid, low], axis=0)


def iota(shape, dim):
    return lax.broadcasted_iota(jnp.int32, shape, dim)


def kernel(
    ns, nc, planes, tiles,
    state_h, forcing_h, inverse_h, lower_h, upper_h, coupling_h, blank_h,
    receiver_r, block_s, offset_r, weight_r, target_r,
    final_h, update_h,
    state, forcing, inverse, lower, upper, coupling, blank,
    drive, near, update, gathered, placed, outgoing, received, pick, stacked,
    edge_out, edge_in,
    stage, mats, comp, all_m, all_b, all_g,
    zero, chip_b, chip_c, x_in, x_out, x_face, g_own, g_inner, y_in, y_out, y_face,
    load_sem, out_sem, fsend, frecv, esend, erecv, msend, mrecv, csend, crecv,
    asend, arecv, dsend, drecv,
):
    s, c = lax.axis_index("stream"), lax.axis_index("cross")
    devices = ns * nc
    me = s * nc + c
    senders = block_s.shape[0]
    slots = devices * CAP
    groups = ns // 2
    half = tiles // 2
    core = lax.rem(s, 2)
    group = s // 2
    first, last = group == 0, group == groups - 1
    even = lax.rem(group, 2) == 0
    own_base = lax.rem(core + group, 2) * half
    far_base = half - own_base

    loads = []

    def load(source, target):
        copy = pltpu.make_async_copy(source, target, load_sem.at[len(loads)])
        copy.start()
        loads.append(copy)
        return copy

    def rows_of(i):
        return pl.ds(i * tiles, tiles)

    sweep_loads = []
    for i in range(planes):
        sweep_loads.append(load(lower_h.at[:, :, i, :], lower.at[:, rows_of(i), :]))
        for a in range(NV):
            top = pair(a, a)
            sweep_loads.append(
                load(
                    inverse_h.at[a, pl.ds(a, NV - a), :, i, :],
                    inverse.at[pl.ds(top, NV - a), rows_of(i), :],
                )
            )
    upper_loads = []
    for i in range(planes):
        upper_loads.append(load(upper_h.at[:, :, i, :], upper.at[:, rows_of(i), :]))
    barrier = pltpu.get_barrier_semaphore()

    def greet(k, carry):
        other = lax.rem(me + k, devices)
        pl.semaphore_signal(
            barrier, inc=1, device_id=(other // nc, lax.rem(other, nc)), device_id_type=MESH
        )
        return carry

    lax.fori_loop(1, devices, greet, 0)

    state_loads = [load(state_h.at[:, :, i, :], state.at[:, rows_of(i), :]) for i in range(planes)]
    drive_loads = []
    for i in range(planes):
        drive_loads.append(load(forcing_h.at[:, :, i, :], forcing.at[:, rows_of(i), :]))
        drive_loads.append(load(coupling_h.at[:, i, :], coupling.at[rows_of(i), :]))
        drive_loads.append(load(blank_h.at[:, i, :], blank.at[rows_of(i), :]))

    eye = iota((senders, senders), 0) == iota((senders, senders), 1)
    recv_row = receiver_r[...].astype(jnp.float32)
    recv_col = jnp.sum(jnp.where(eye, recv_row, 0.0), axis=1, keepdims=True)
    earlier = iota((senders, senders), 0) < iota((senders, senders), 1)
    rank_row = jnp.sum(
        jnp.where(earlier & (recv_col == recv_row), 1.0, 0.0), axis=0, keepdims=True
    )
    key_row = rank_row * devices + recv_row
    place = (key_row == iota((slots, senders), 0).astype(jnp.float32)).astype(jnp.float32)
    place3 = jnp.concatenate([place, place, place], axis=1).astype(jnp.bfloat16)
    offset_col = jnp.sum(
        jnp.where(eye, offset_r[...].astype(jnp.float32), 0.0), axis=1, keepdims=True
    ).astype(jnp.int32)
    offset_all = jnp.broadcast_to(offset_col, (senders, 128))

    def fill_pick():
        slot_eye = iota((slots, slots), 0) == iota((slots, slots), 1)
        target_col = jnp.sum(
            jnp.where(slot_eye, target_r[...].astype(jnp.float32), 0.0), axis=1, keepdims=True
        )
        slot_k = iota((slots, slots), 1)
        wanted = jnp.where(slot_k < devices, slot_k * CAP, (slot_k - devices) * CAP + 1)
        target_row = jnp.sum(
            jnp.where(iota((slots, slots), 0) == wanted, target_col, 0.0), axis=0, keepdims=True
        )
        target3 = jnp.concatenate([target_row, target_row, target_row], axis=1)

        def fill(i, carry):
            ids = (iota((tiles, 3 * slots), 0) + i * tiles).astype(jnp.float32)
            pick[pl.ds(pl.multiple_of(i * tiles, tiles), tiles), :] = jnp.where(
                ids == target3, 1.0, 0.0
            ).astype(jnp.bfloat16)
            return carry

        lax.fori_loop(0, planes, fill, 0)

    def fringe_copy(it, k):
        other = lax.rem(me + k, devices)
        start = pl.multiple_of(other * SLOT_ROWS, SLOT_ROWS)
        mine = pl.multiple_of(me * SLOT_ROWS, SLOT_ROWS)
        return pltpu.make_async_remote_copy(
            src_ref=outgoing.at[it, pl.ds(start, NV * CAP), :],
            dst_ref=received.at[it, pl.ds(mine, NV * CAP), :],
            send_sem=fsend.at[it, k],
            recv_sem=frecv.at[it, k],
            device_id=(other // nc, lax.rem(other, nc)),
            device_id_type=MESH,
        )

    def edge_copy(it, side):
        other = lax.rem(c + 1, nc) if side == 0 else lax.rem(c + nc - 1, nc)
        return pltpu.make_async_remote_copy(
            src_ref=edge_out.at[it, side],
            dst_ref=edge_in.at[it, side],
            send_sem=esend.at[it, side],
            recv_sem=erecv.at[it, side],
            device_id=(s, other),
            device_id_type=MESH,
        )

    def member(other_group, across):
        return other_group * 2 + (1 - core if across else core)

    partner = member(group, True)
    parts = [pl.ds(k * PART, PART) for k in range(half // PART)]

    def face_copy(it, kind, way, source, target, to):
        return pltpu.make_async_remote_copy(
            src_ref=source,
            dst_ref=target,
            send_sem=csend.at[it, way],
            recv_sem=crecv.at[it, kind],
            device_id=(to, c),
            device_id_type=MESH,
        )

    def mats_copy(k):
        third = pl.ds(k * MATS, MATS)
        return pltpu.make_async_remote_copy(
            src_ref=mats.at[2, third],
            dst_ref=mats.at[core, third],
            send_sem=msend.at[k],
            recv_sem=mrecv.at[k],
            device_id=(partner, c),
            device_id_type=MESH,
        )

    def chip_copy(kind, piece, sender, d):
        first_row, size = piece
        away = d if kind == 0 else -d
        return pltpu.make_async_remote_copy(
            src_ref=comp.at[pl.ds(kind * MATS + first_row, size)],
            dst_ref=all_m.at[kind, sender, pl.ds(first_row, size)],
            send_sem=asend.at[kind, PIECES.index(piece), d],
            recv_sem=arecv.at[kind, PIECES.index(piece), sender],
            device_id=(member(group + away, d % 2 == 1), c),
            device_id_type=MESH,
        )

    def chip_to(kind, d):
        inside = (group > 0) & (group < groups - 1)
        return inside & ((group + d < groups) if kind == 0 else (group >= d))

    def pass_copy(kind, piece, owner):
        rows = pl.ds(piece[0], piece[1])
        source = all_m.at[kind, owner, rows]
        return pltpu.make_async_remote_copy(
            src_ref=source,
            dst_ref=source,
            send_sem=asend.at[kind, PIECES.index(piece), 0],
            recv_sem=arecv.at[kind, PIECES.index(piece), owner],
            device_id=(member(group + (1 if kind else -1), True), c),
            device_id_type=MESH,
        )

    def passes(kind):
        return (even & (group < groups - 2)) if kind else (jnp.logical_not(even) & (group > 1))

    def wait_chip(kind, owner):
        for piece in PIECES:
            chip_copy(kind, piece, owner, 1).wait_recv()

    def wait_mats(kind):
        end = first if kind else last
        for i in range(1, groups - 1):
            due = (group < i) if kind else (group > i)
            passed = passes(kind) & (group == (i - 2 if kind else i + 2)) & jnp.logical_not(end)

            @pl.when(due & jnp.logical_not(passed))
            def _():
                wait_chip(kind, i)

    def pass_on(kind):
        end = first if kind else last
        owner = group + (2 if kind else -2)

        @pl.when(passes(kind))
        def _():
            @pl.when(jnp.logical_not(end))
            def _():
                wait_chip(kind, owner)

            for piece in PIECES:
                pass_copy(kind, piece, owner).start()

    def send_chip(kind, d, pieces, extra):
        @pl.when(chip_to(kind, d) & extra)
        def _():
            for piece in pieces:
                chip_copy(kind, piece, group, d).start()

    def direct_copy(it, kind, sender, d, k):
        rows = parts[k]
        source, target = ((chip_b, all_b), (g_own, all_g))[kind]
        away = d if kind == 0 else -d
        return pltpu.make_async_remote_copy(
            src_ref=source.at[it, :, rows, :],
            dst_ref=target.at[it, sender, :, rows, :],
            send_sem=dsend.at[it, kind, d, k],
            recv_sem=drecv.at[it, kind, sender, k],
            device_id=(member(group + away, d % 2 == 1), c),
            device_id_type=MESH,
        )

    def direct_to(it, kind, d):
        if it == 0:
            return (group + d == groups - 1) if kind == 0 else (group == d)
        return (group + d < groups) if kind == 0 else (group >= d)

    def send_direct(it, kind, k):
        for d in reversed(range(1, groups)):
            @pl.when(direct_to(it, kind, d))
            def _():
                direct_copy(it, kind, group, d, k).start()

    def b_to_partner(it):
        return face_copy(it, 0, 0, zero.at[it, 2, 0], zero.at[it, core, 0], partner)

    def c_to_partner(it):
        return face_copy(it, 1, 1, zero.at[it, 2, 1], zero.at[it, core, 1], partner)

    def x_to_next(it, k, source):
        rows = parts[k]
        return face_copy(
            it, 2 + k, 2 + k, source.at[it, :, rows, :], x_in.at[it, :, rows, :], member(group + 1, True)
        )

    def y_to_prev(it, k):
        rows = parts[k]
        n = 2 + len(parts) + k
        return face_copy(
            it, n, n, y_out.at[it, :, rows, :], y_in.at[it, :, rows, :], member(group - 1, True)
        )

    own_rows = pl.ds(pl.multiple_of(own_base, half), half)

    def x_to_partner(it):
        source = x_face.at[it, 1 - core, :, own_rows, :]
        n = 2 + 2 * len(parts)
        return face_copy(it, n, n, source, source, partner)

    def y_to_partner(it, k, send):
        side, base = (1 - core, own_base) if send else (core, far_base)
        rows = pl.ds(pl.multiple_of(base + k * PART, PART), PART)
        source = y_face.at[it, side, :, rows, :]
        n = 3 + 2 * len(parts) + k
        return face_copy(it, n, n, source, source, partner)

    def block(rows):
        return [inverse[k, rows, :] for k in range(len(PAIRS))]

    def dot(terms):
        total = None
        for left, right in terms:
            total = left * right if total is None else total + left * right
        return total

    def apply(blocks, vector):
        return [dot([(blocks[pair(a, b)], vector[b]) for b in range(NV)]) for a in range(NV)]

    def at(base, size):
        return pl.ds(pl.multiple_of(base, 8), size)

    def matrix(ref, first, rows):
        return [[ref[first + a * NV + b, rows, :] for b in range(NV)] for a in range(NV)]

    def times(rows_of_matrix, vector):
        return [dot([(rows_of_matrix[a][b], vector[b]) for b in range(NV)]) for a in range(NV)]

    def column(m, b):
        return [m[a][b] for a in range(NV)]

    def send_donors(it):
        for v in range(NV):
            edge_out[it, 0, v] = state[v, pl.ds(tiles - 1, planes, stride=tiles), :]
            edge_out[it, 1, v] = state[v, pl.ds(0, planes, stride=tiles), :]
        for side in range(2):
            edge_copy(it, side).start()

        def gather(q, carry):
            for k in range(8):
                e = q * 8 + k
                chosen = block_s[e]
                for v in range(NV):
                    gathered[v, pl.ds(e, 1), :] = state[v, pl.ds(chosen, 1), :]
            return carry

        lax.fori_loop(0, senders // 8, gather, 0)
        weight = weight_r[...]
        for v in range(NV):
            chosen = gathered[v]
            moved = chosen
            for bit in range(7):
                rolled = pltpu.roll(moved, 128 - (1 << bit), 1)
                moved = jnp.where((offset_all & (1 << bit)) != 0, rolled, moved)
            placed[:, v * 128:(v + 1) * 128] = split3(weight * (chosen + moved))
        slot_values = jnp.dot(place3, placed[...], preferred_element_type=jnp.float32)
        for v in range(NV):
            for k in range(CAP):
                outgoing[it, pl.ds(v * CAP + k, devices, stride=SLOT_ROWS), :] = slot_values[
                    k * devices:(k + 1) * devices, v * 128:(v + 1) * 128
                ]

        def send(k, carry):
            fringe_copy(it, k).start()
            return carry

        lax.fori_loop(1, devices, send, 0)
        mine = pl.ds(pl.multiple_of(me * SLOT_ROWS, SLOT_ROWS), NV * CAP)
        received[it, mine, :] = outgoing[it, mine, :]

    each = half // 8

    def place_of(q):
        local = lax.rem(q, each) * 8
        base = jnp.where(q < each, far_base, own_base) + local
        return base, jnp.where(q < each, 2, core), at(local, 8)

    def keep(k, slot, spot, columns):
        for b in range(NV):
            for a in range(NV):
                mats[slot, k * MATS + a * NV + b, spot, :] = columns[b][a]

    def advance(blocks, factor, columns):
        if columns is None:
            return [[blocks[pair(a, b)] * factor[b] for a in range(NV)] for b in range(NV)]
        return [apply(blocks, [factor[v] * columns[b][v] for v in range(NV)]) for b in range(NV)]

    def transfer_a(q, carry):
        base, slot, spot = place_of(q)
        chain = None
        for i in range(planes):
            rows = at(i * tiles + base, 8)
            chain = advance(block(rows), [lower[v, rows, :] for v in range(NV)], chain)
            for b in range(NV):
                for a in range(NV):
                    stage[i, a * NV + b, at(base, 8), :] = chain[b][a]
        keep(0, slot, spot, chain)

        @pl.when(q == each - 1)
        def _():
            for copy in state_loads:
                copy.wait()
            pl.semaphore_wait(barrier, devices - 1)
            send_donors(0)
            mats_copy(0).start()

        return carry

    def transfer_e(q, carry):
        base, slot, spot = place_of(q)
        back = None
        for i in reversed(range(planes)):
            rows = at(i * tiles + base, 8)
            back = advance(block(rows), [upper[v, rows, :] for v in range(NV)], back)
        keep(1, slot, spot, back)

        @pl.when(q == each - 1)
        def _():
            mats_copy(1).start()

        return carry

    def transfer_d(q, carry):
        base, slot, spot = place_of(q)
        spot_all = at(base, 8)
        both = [
            [stage[planes - 1, a * NV + b, spot_all, :] for a in range(NV)] for b in range(NV)
        ]
        for i in reversed(range(planes - 1)):
            rows = at(i * tiles + base, 8)
            both = advance(block(rows), [upper[v, rows, :] for v in range(NV)], both)
            both = [
                [stage[i, a * NV + b, spot_all, :] + both[b][a] for a in range(NV)]
                for b in range(NV)
            ]
        keep(2, slot, spot, both)

        @pl.when(q == each - 1)
        def _():
            mats_copy(2).start()

        return carry

    def compose_a(q, carry):
        rows = at(q * 8, 8)
        low_a = matrix(mats.at[0], 0, rows)
        high_a = matrix(mats.at[1], 0, rows)
        for b in range(NV):
            out = times(high_a, column(low_a, b))
            for a in range(NV):
                comp[a * NV + b, rows, :] = out[a]
        return carry

    def compose_e(q, carry):
        rows = at(q * 8, 8)
        low_e = matrix(mats.at[0], MATS, rows)
        high_e = matrix(mats.at[1], MATS, rows)
        for b in range(NV):
            out = times(low_e, column(high_e, b))
            for a in range(NV):
                comp[MATS + a * NV + b, rows, :] = out[a]
        return carry

    def compose_d(q, carry):
        rows = at(q * 8, 8)
        low_a = matrix(mats.at[0], 0, rows)
        low_e = matrix(mats.at[0], MATS, rows)
        high_d = matrix(mats.at[1], 2 * MATS, rows)
        for b in range(NV):
            out = times(low_e, times(high_d, column(low_a, b)))
            for a in range(NV):
                k = 2 * MATS + a * NV + b
                comp[k, rows, :] = mats[0, k, rows, :] + out[a]
        return carry

    def send_matrices(kind):
        for d in range(2, groups):
            send_chip(kind, d, PIECES, True)
        send_chip(kind, 1, PIECES, jnp.logical_not(even) if kind else even)

    def zero_down(it, base, slot):
        for g in range(half // STEP):
            x = None
            for i in range(planes):
                rows = at(i * tiles + base + g * STEP, STEP)
                t = [drive[v, rows, :] for v in range(NV)]
                if x is not None:
                    t = [t[v] + lower[v, rows, :] * x[v] for v in range(NV)]
                x = apply(block(rows), t)
                for v in range(NV):
                    near[v, rows, :] = x[v]
            for v in range(NV):
                zero[it, slot, 0, v, pl.ds(g * STEP, STEP), :] = x[v]

    def zero_up(it, base, slot):
        for g in range(half // STEP):
            rows = at((planes - 1) * tiles + base + g * STEP, STEP)
            y = [near[v, rows, :] for v in range(NV)]
            for i in reversed(range(planes - 1)):
                rows = at(i * tiles + base + g * STEP, STEP)
                z = apply(block(rows), [upper[v, rows, :] * y[v] for v in range(NV)])
                y = [near[v, rows, :] + z[v] for v in range(NV)]
            for v in range(NV):
                zero[it, slot, 1, v, pl.ds(g * STEP, STEP), :] = y[v]

    def true_down(it, base):
        for g in range(half // STEP):
            x = [x_face[it, core, v, at(base + g * STEP, STEP), :] for v in range(NV)]
            for i in range(planes):
                rows = at(i * tiles + base + g * STEP, STEP)
                t = [drive[v, rows, :] + lower[v, rows, :] * x[v] for v in range(NV)]
                x = apply(block(rows), t)
                for v in range(NV):
                    near[v, rows, :] = x[v]

    def true_up(it, base):
        for g in range(half // STEP):
            y = [y_face[it, core, v, at(base + g * STEP, STEP), :] for v in range(NV)]
            for i in reversed(range(planes)):
                rows = at(i * tiles + base + g * STEP, STEP)
                z = apply(block(rows), [upper[v, rows, :] * y[v] for v in range(NV)])
                y = [near[v, rows, :] + z[v] for v in range(NV)]
                for v in range(NV):
                    if it == ITERS - 1:
                        update[v, rows, :] = y[v]
                    state[v, rows, :] = state[v, rows, :] + y[v]

    def out_copies(part, base):
        copies = []
        for i in range(planes):
            rows = pl.ds(pl.multiple_of(i * tiles + base, half), half)
            cells = pl.ds(pl.multiple_of(base, half), half)
            for n, (source, target) in enumerate(((state, final_h), (update, update_h))):
                copies.append(
                    pltpu.make_async_copy(
                        source.at[:, rows, :], target.at[:, cells, i, :], out_sem.at[part, i, n]
                    )
                )
        return copies

    steps = [pl.ds(g * STEP, STEP) for g in range(half // STEP)]

    def chip_forward(it):
        for rows in steps:
            low = [zero[it, 0, 0, v, rows, :] for v in range(NV)]
            out = times(matrix(mats.at[1], 0, rows), low)
            for v in range(NV):
                chip_b[it, v, rows, :] = zero[it, 1, 0, v, rows, :] + out[v]

    def chip_backward(it):
        for rows in steps:
            low = [zero[it, 0, 0, v, rows, :] for v in range(NV)]
            out = times(matrix(mats.at[1], 2 * MATS, rows), low)
            out = [out[v] + zero[it, 1, 1, v, rows, :] for v in range(NV)]
            out = times(matrix(mats.at[0], MATS, rows), out)
            for v in range(NV):
                chip_c[it, v, rows, :] = zero[it, 0, 1, v, rows, :] + out[v]

    def own(g):
        return at(own_base + g * STEP, STEP)

    def relay_forward(it):
        for k, rows in enumerate(parts):
            @pl.when(jnp.logical_not(first))
            def _():
                x_to_next(it, k, x_out).wait_recv()

            x = [x_in[it, v, rows, :] for v in range(NV)]
            out = times(matrix(comp, 0, rows), x)
            for v in range(NV):
                x_out[it, v, rows, :] = chip_b[it, v, rows, :] + out[v]
                x_face[it, 0, v, at(own_base + k * PART, PART), :] = x[v]

            @pl.when((group > 0) & (group < groups - 2))
            def _():
                x_to_next(it, k, x_out).start()

    def turn(it, k):
        rows = parts[k]
        x = [x_face[it, 0, v, at(own_base + k * PART, PART), :] for v in range(NV)]
        out = times(matrix(comp, 2 * MATS, rows), x)
        for v in range(NV):
            g_own[it, v, rows, :] = chip_c[it, v, rows, :] + out[v]

    def inner_forward(it):
        for g, rows in enumerate(steps):
            x = [x_face[it, 0, v, own(g), :] for v in range(NV)]
            out = times(matrix(mats.at[0], 0, rows), x)
            high = [zero[it, 0, 0, v, rows, :] + out[v] for v in range(NV)]
            out = times(matrix(mats.at[1], 2 * MATS, rows), high)
            for v in range(NV):
                x_face[it, 1, v, own(g), :] = high[v]
                g_inner[it, v, rows, :] = zero[it, 1, 1, v, rows, :] + out[v]

    def relay_backward(it):
        for k, rows in enumerate(parts):
            @pl.when(jnp.logical_not(last))
            def _():
                y_to_prev(it, k).wait_recv()

            y = [y_in[it, v, rows, :] for v in range(NV)]
            out = times(matrix(comp, MATS, rows), y)
            for v in range(NV):
                y_out[it, v, rows, :] = g_own[it, v, rows, :] + out[v]

            @pl.when(group > 1)
            def _():
                y_to_prev(it, k).start()

            mine = at(own_base + k * PART, PART)
            back = times(matrix(mats.at[1], MATS, rows), y)
            for v in range(NV):
                y_face[it, 1, v, mine, :] = y[v]
                y_face[it, 0, v, mine, :] = g_inner[it, v, rows, :] + back[v]
            y_to_partner(it, k, True).start()

    def direct_face(it, kind, k):
        source, face, side = ((all_b, x_face, 0), (all_g, y_face, 1))[kind]
        far = 0 if kind == 0 else groups - 1
        mine = (group > 0) if kind == 0 else (group < groups - 1)
        rows, spot = parts[k], at(own_base + k * PART, PART)

        @pl.when(jnp.logical_not(mine))
        def _():
            face[it, side, :, spot, :] = jnp.zeros((NV, PART, 128), jnp.float32)

        @pl.when(mine)
        def _():
            direct_copy(it, kind, far, 1, k).wait_recv()
            face[it, side, :, spot, :] = source[it, far, :, rows, :]

        inner = range(1, groups - 1)
        for i in inner if kind == 0 else reversed(inner):
            @pl.when((group > i) if kind == 0 else (group < i))
            def _():
                direct_copy(it, kind, i, 1, k).wait_recv()
                x = [face[it, side, v, spot, :] for v in range(NV)]
                out = times(matrix(all_m.at[kind, i], 0, rows), x)
                for v in range(NV):
                    face[it, side, v, spot, :] = source[it, i, v, rows, :] + out[v]

    def direct_forward(it):
        for k in range(len(parts)):
            direct_face(it, 0, k)
            turn(it, k)
            send_direct(it, 1, k)

    def direct_backward(it):
        for k, rows in enumerate(parts):
            direct_face(it, 1, k)
            mine = at(own_base + k * PART, PART)
            y = [y_face[it, 1, v, mine, :] for v in range(NV)]
            back = times(matrix(mats.at[1], MATS, rows), y)
            for v in range(NV):
                y_face[it, 0, v, mine, :] = g_inner[it, v, rows, :] + back[v]
            y_to_partner(it, k, True).start()

    face_zero = jnp.zeros((NV, half, 128), jnp.float32)

    @pl.when(first)
    def _():
        x_in[0] = face_zero

    @pl.when(last)
    def _():
        y_in[0] = face_zero

    for it in range(ITERS):
        if it > 0:
            send_donors(it)
        if it == 0:
            fill_pick()
            for copy in sweep_loads:
                copy.wait()
            lax.fori_loop(0, tiles // 8, transfer_a, 0)
            mats_copy(0).wait_recv()
            lax.fori_loop(0, each, compose_a, 0)
            send_matrices(0)
            for copy in upper_loads:
                copy.wait()
            lax.fori_loop(0, tiles // 8, transfer_e, 0)
            mats_copy(1).wait_recv()
            lax.fori_loop(0, each, compose_e, 0)
            send_matrices(1)
            for copy in drive_loads:
                copy.wait()
        lane = iota((tiles, 128), 1)
        row = iota((tiles, 128), 0)

        def drive_plane(i, carry):
            rows = pl.ds(pl.multiple_of(i * tiles, tiles), tiles)
            factor = coupling[rows, :]
            for v in range(NV):
                x = state[v, rows, :]
                left = pltpu.roll(x, 1, 1)
                left = jnp.where(
                    lane == 0, jnp.where(row == 0, 0.0, pltpu.roll(left, 1, 0)), left
                )
                right = pltpu.roll(x, 127, 1)
                right = jnp.where(
                    lane == 127,
                    jnp.where(row == tiles - 1, 0.0, pltpu.roll(right, tiles - 1, 0)),
                    right,
                )
                drive[v, rows, :] = forcing[v, rows, :] - factor * (2.0 * x - left - right)
            return carry

        lax.fori_loop(0, planes, drive_plane, 0)
        for side in range(2):
            edge_copy(it, side).wait_recv()
            rows = pl.ds(0 if side == 0 else tiles - 1, planes, stride=tiles)
            hit = iota((planes, 128), 1) == (0 if side == 0 else 127)
            for v in range(NV):
                beyond = pltpu.roll(edge_in[it, side, v], 1 if side == 0 else 127, 1)
                drive[v, rows, :] = drive[v, rows, :] + coupling[rows, :] * jnp.where(
                    hit, beyond, 0.0
                )

        def take(k, carry):
            fringe_copy(it, k).wait_recv()
            return carry

        lax.fori_loop(1, devices, take, 0)
        for v in range(NV):
            pieces = [
                received[it, pl.ds(v * CAP + k, devices, stride=SLOT_ROWS), :] for k in range(CAP)
            ]
            stacked[:, v * 128:(v + 1) * 128] = split3(jnp.concatenate(pieces, axis=0))

        def add_fringe(i, carry):
            rows = pl.ds(pl.multiple_of(i * tiles, tiles), tiles)
            hole = (1 - blank[rows, :]).astype(jnp.float32)
            fringe = jnp.dot(pick[rows, :], stacked[...], preferred_element_type=jnp.float32)
            for v in range(NV):
                drive[v, rows, :] = drive[v, rows, :] + hole * fringe[:, v * 128:(v + 1) * 128]
            return carry

        lax.fori_loop(0, planes, add_fringe, 0, unroll=True)

        zero_down(it, far_base, 2)
        b_to_partner(it).start()
        zero_down(it, own_base, core)
        b_to_partner(it).wait_recv()
        chip_forward(it)

        if it == 0:
            @pl.when(first)
            def _():
                for k in range(len(parts)):
                    x_to_next(it, k, chip_b).start()

        for k in range(len(parts)):
            send_direct(it, 0, k)

        zero_up(it, far_base, 2)
        c_to_partner(it).start()
        zero_up(it, own_base, core)
        if it == 0:
            @pl.when((group > 0) & (group < groups - 2))
            def _():
                relay_forward(it)

            lax.fori_loop(0, tiles // 8, transfer_d, 0)
            mats_copy(2).wait_recv()
            lax.fori_loop(0, each, compose_d, 0)
        c_to_partner(it).wait_recv()
        chip_backward(it)
        if it == 0:
            @pl.when(last)
            def _():
                wait_mats(0)
                direct_forward(it)

            @pl.when(first | (group == groups - 2))
            def _():
                relay_forward(it)

            @pl.when(jnp.logical_not(last))
            def _():
                for k in range(len(parts)):
                    turn(it, k)
                    send_direct(it, 1, k)
        else:
            @pl.when(jnp.logical_not(last))
            def _():
                wait_mats(0)

            direct_forward(it)
        inner_forward(it)
        if it == 0:
            @pl.when(last)
            def _():
                relay_backward(it)

        x_to_partner(it).start()
        true_down(it, own_base)
        x_to_partner(it).wait_recv()
        true_down(it, far_base)
        if it == 0:
            @pl.when(first)
            def _():
                wait_mats(1)

            pass_on(1)

            @pl.when(first)
            def _():
                direct_backward(it)

            @pl.when(jnp.logical_not(first | last))
            def _():
                relay_backward(it)
        else:
            @pl.when(jnp.logical_not(first))
            def _():
                wait_mats(1)

            direct_backward(it)
        true_up(it, own_base)
        if it == ITERS - 1:
            for copy in out_copies(0, own_base):
                copy.start()
        for k in range(len(parts)):
            y_to_partner(it, k, False).wait_recv()
        true_up(it, far_base)
        if it == 0:
            pass_on(0)
        if it == ITERS - 1:
            for copy in out_copies(1, far_base):
                copy.start()

    for kind in range(2):
        @pl.when(passes(kind))
        def _():
            for piece in PIECES:
                pass_copy(kind, piece, group).wait_send()

        for d in range(1, groups):
            near_by = True if d > 1 else (jnp.logical_not(even) if kind else even)

            @pl.when(chip_to(kind, d) & near_by)
            def _():
                for piece in PIECES:
                    chip_copy(kind, piece, group, d).wait_send()

            for it in range(ITERS):
                @pl.when(direct_to(it, kind, d))
                def _():
                    for k in range(len(parts)):
                        direct_copy(it, kind, group, d, k).wait_send()

    for k in range(3):
        mats_copy(k).wait_send()

    for it in range(ITERS):
        for side in range(2):
            edge_copy(it, side).wait_send()

        def sent(k, carry):
            fringe_copy(it, k).wait_send()
            return carry

        lax.fori_loop(1, devices, sent, 0)
        b_to_partner(it).wait_send()
        c_to_partner(it).wait_send()
        x_to_partner(it).wait_send()
        for k in range(len(parts)):
            y_to_partner(it, k, True).wait_send()

        if it > 0:
            continue

        @pl.when(group < groups - 2)
        def _():
            for k in range(len(parts)):
                x_to_next(it, k, x_out).wait_send()

        @pl.when(group > 1)
        def _():
            for k in range(len(parts)):
                y_to_prev(it, k).wait_send()

    for part, base in enumerate((own_base, far_base)):
        for copy in out_copies(part, base):
            copy.wait()


def shards(
    initial_state, forcing, block_inverse, lower_decay, upper_decay, cross_coupling, iblank,
    donor_receiver, donor_block, stencil_offset, stencil_weight, fringe_target,
):
    ns, nc = lax.axis_size("stream"), lax.axis_size("cross")
    devices = ns * nc
    planes, cells = initial_state.shape[1:]
    tiles = cells // 128
    senders = donor_block.shape[0]
    slots = devices * CAP

    def tiled(x):
        lead = x.shape[:-2]
        n = len(lead)
        order = tuple(range(n)) + (n + 1, n, n + 2)
        return x.reshape(lead + (planes, tiles, 128)).transpose(order)

    def untiled(x):
        return x.transpose(0, 2, 1, 3).reshape(NV, planes, cells)

    full = (NV, planes * tiles, 128)
    half = tiles // 2
    groups = ns // 2
    f32, bf16 = jnp.float32, jnp.bfloat16
    dma = pltpu.SemaphoreType.DMA
    face = pltpu.VMEM((ITERS, NV, half, 128), f32)
    out = jax.ShapeDtypeStruct((NV, tiles, planes, 128), f32)
    hbm = pl.BlockSpec(memory_space=pl.ANY)
    vmem = pl.BlockSpec(memory_space=pltpu.VMEM)
    smem = pl.BlockSpec(memory_space=pltpu.SMEM)
    final, update = pl.pallas_call(
        functools.partial(kernel, ns, nc, planes, tiles),
        out_shape=(out, out),
        in_specs=[hbm] * 7 + [vmem, smem, vmem, vmem, vmem],
        out_specs=(hbm, hbm),
        scratch_shapes=[
            pltpu.VMEM(full, f32),
            pltpu.VMEM(full, f32),
            pltpu.VMEM((len(PAIRS),) + full[1:], f32),
            pltpu.VMEM(full, f32),
            pltpu.VMEM(full, f32),
            pltpu.VMEM(full[1:], f32),
            pltpu.VMEM(full[1:], jnp.int32),
            pltpu.VMEM(full, f32),
            pltpu.VMEM(full, f32),
            pltpu.VMEM(full, f32),
            pltpu.VMEM((NV, senders, 128), f32),
            pltpu.VMEM((3 * senders, NV * 128), bf16),
            pltpu.VMEM((ITERS, devices * SLOT_ROWS, 128), f32),
            pltpu.VMEM((ITERS, devices * SLOT_ROWS, 128), f32),
            pltpu.VMEM((planes * tiles, 3 * slots), bf16),
            pltpu.VMEM((3 * slots, NV * 128), bf16),
            pltpu.VMEM((ITERS, 2, NV, planes, 128), f32),
            pltpu.VMEM((ITERS, 2, NV, planes, 128), f32),
            pltpu.VMEM((planes, MATS, tiles, 128), f32),
            pltpu.VMEM((3, 3 * MATS, half, 128), f32),
            pltpu.VMEM((3 * MATS, half, 128), f32),
            pltpu.VMEM((2, groups, MATS, half, 128), f32),
            pltpu.VMEM((ITERS, groups, NV, half, 128), f32),
            pltpu.VMEM((ITERS, groups, NV, half, 128), f32),
            pltpu.VMEM((ITERS, 3, 2, NV, half, 128), f32),
            face,
            face,
            face,
            face,
            pltpu.VMEM((ITERS, 2, NV, tiles, 128), f32),
            face,
            face,
            face,
            face,
            pltpu.VMEM((ITERS, 2, NV, tiles, 128), f32),
            dma((planes * (4 + 2 + NV),)),
            dma((2, planes, 2)),
            dma((ITERS, devices)),
            dma((ITERS, devices)),
            dma((ITERS, 2)),
            dma((ITERS, 2)),
            dma((3,)),
            dma((3,)),
            dma((ITERS, 3 + 3 * (half // PART))),
            dma((ITERS, 3 + 3 * (half // PART))),
            dma((2, len(PIECES), groups)),
            dma((2, len(PIECES), groups)),
            dma((ITERS, 2, groups, half // PART)),
            dma((ITERS, 2, groups, half // PART)),
        ],
        compiler_params=pltpu.CompilerParams(
            collective_id=0, has_side_effects=True, vmem_limit_bytes=56 * 1024 * 1024
        ),
    )(
        tiled(initial_state), tiled(forcing), tiled(block_inverse), tiled(lower_decay),
        tiled(upper_decay), tiled(cross_coupling), tiled(iblank),
        donor_receiver.reshape(1, senders), donor_block, stencil_offset.reshape(1, senders), stencil_weight,
        fringe_target.reshape(1, slots),
    )
    return untiled(final), untiled(update)


def solution(mesh):
    return jax.shard_map(
        shards,
        mesh=mesh,
        in_specs=(
            P(None, "stream", "cross"),
            P(None, "stream", "cross"),
            P(None, None, "stream", "cross"),
            P(None, "stream", "cross"),
            P(None, "stream", "cross"),
            P("stream", "cross"),
            P("stream", "cross"),
            P(("stream", "cross"), None),
            P(("stream", "cross")),
            P(("stream", "cross")),
            P(("stream", "cross"), None),
            P(("stream", "cross")),
        ),
        out_specs=(P(None, "stream", "cross"), P(None, "stream", "cross")),
        check_vma=False,
    )
```
